1024 devices in a mesh: exp: 8 (over y, core), et: 128 (over x, z).
Axes of the slice: x: 4, y: 4, z: 32, core: 2. Of those that a mesh axis runs over, the one named last changes fastest.
Arguments:
- grad_out: bfloat16 [1024, 4096], P(('exp', 'et')), may hold values from -3 to 3
- route_weight: bfloat16 [1024, 8], P(('exp', 'et')), may hold values from 0.099609375 to 1
- expert_ids: int32 [1024, 8], P(('exp', 'et')), may hold values from 0 to 63, as said below
- slot_ids: int32 [1024, 8], P(('exp', 'et')), may hold values from 0 to 29, as said below
- saved_pre: bfloat16 [1024, 240, 192], P(('exp', 'et')), may hold values from -6 to 6
- gate_proj: bfloat16 [1024, 96, 4096], P(('exp', 'et')), may hold values from -0.09375 to 0.09375
- up_proj: bfloat16 [1024, 96, 4096], P(('exp', 'et')), may hold values from -0.09375 to 0.09375
- down_proj: bfloat16 [1024, 96, 4096], P(('exp', 'et')), may hold values from -0.15625 to 0.15625
Outputs:
- grad_tokens: bfloat16 [1024, 4096], P(('exp', 'et'))
- grad_weights: float32 [1024, 8], P(('exp', 'et'))
- grad_down: bfloat16 [1024, 96, 4096], P(('exp', 'et'))
The draws below stay inside these ranges and needn't reach their ends.
Inputs may be any that keep to these rules, and one draw needn't show every extreme that they name: `expert_ids`: each token names 8 different experts. Among the tokens of each aligned block of 128 tokens (one index of exp), every expert is named 2 to 30 times, and one expert, the same in every block, is named exactly 30 times. slot_ids[t, k] is the rank of choice (t, k) among the choices of its block that name the same expert, counted by token and then by choice.
All inputs are finite; a program needn't handle non-finite values.
Results may differ from the reference program's by a relative error of at most 0.02.
Values may be sent and summed in bfloat16 or wider, within the bound.
A program may use at most 64 MiB of HBM per device.

```python
import math
import jax
import jax.numpy as jnp
from jax import lax

D = 4096
FF = 1536
TOPK = 8
HID_SPLIT = 16
FF_DEV = 96
EXPERTS = 64
TOK_ROW = 128
TOKENS = 1024
CAP = 30
SLOTS = 240
N_EXP = 8


def route_tables(key):
    full_key, block_key = jax.random.split(key)
    full_expert = jax.random.randint(full_key, (), 0, EXPERTS)
    block_keys = jax.random.split(block_key, N_EXP)
    pair_total = 2 * (TOK_ROW * TOPK // EXPERTS)

    def one_block(sub_key):
        perm_key, load_key, token_key = jax.random.split(sub_key, 3)
        expert_order = jax.random.permutation(perm_key, EXPERTS)
        leading = expert_order[0]
        index_line = jnp.arange(EXPERTS)
        expert_order = jnp.where(expert_order == full_expert, leading, expert_order)
        expert_order = jnp.where(index_line == 0, full_expert, expert_order)
        pair_loads = jax.random.randint(load_key, (EXPERTS // 2,), pair_total - CAP, CAP + 1)
        pair_loads = pair_loads.at[0].set(CAP)
        paired = jnp.stack([pair_loads, pair_total - pair_loads], axis=1).reshape(EXPERTS)
        bounds = jnp.cumsum(paired)
        entries = jnp.arange(TOK_ROW * TOPK)
        position = jnp.sum((entries[:, None] >= bounds[None, :]).astype(jnp.int32), axis=1)
        listed = expert_order[position]
        route_table = listed.reshape(TOPK, TOK_ROW).T
        shuffle = jax.random.permutation(token_key, TOK_ROW)
        route_table = route_table[shuffle]
        flat_routes = route_table.reshape(-1)
        onehot = (flat_routes[:, None] == jnp.arange(EXPERTS)[None, :]).astype(jnp.int32)
        running = jnp.cumsum(onehot, axis=0) - 1
        slot_table = jnp.sum(running * onehot, axis=1)
        return (route_table, slot_table.reshape(TOK_ROW, TOPK))
    route_tables_all, slot_tables_all = jax.vmap(one_block)(block_keys)
    return (route_tables_all.reshape(TOKENS, TOPK).astype(jnp.int32), slot_tables_all.reshape(TOKENS, TOPK).astype(jnp.int32))


def draw_expert_ids(key, part):
    route_table, slot_table = route_tables(key)
    return route_table


def draw_slot_ids(key, part):
    route_table, slot_table = route_tables(key)
    return slot_table


def steps_of(rng, shape, pieces, least, high):
    def one(dim, blocks):
        heights = jax.random.uniform(jax.random.fold_in(jax.random.fold_in(rng, 6), dim), (blocks,), jnp.float32, least / len(pieces), high / len(pieces))
        return jnp.repeat(jnp.exp(heights), shape[dim] // blocks).reshape((-1,) + (1,) * (len(shape) - dim - 1))

    gain = one(*pieces[0])
    for cut in pieces[1:]:
        gain = gain * one(*cut)
    return gain


def centred(own_key, dims, scale, bound, shards=(), kind=jnp.bfloat16):
    drawn = scale * jax.random.normal(own_key, dims, jnp.float32)
    if shards:
        drawn = drawn * steps_of(own_key, dims, shards, -0.22, 0.18)
    return jnp.clip(drawn, -bound, bound).astype(kind)


def setup_inputs(seed: int = 0) -> dict:
    arg_keys = jax.random.split(jax.random.key(seed), 9)
    return {
        "grad_out": centred(arg_keys[0], (TOKENS, D), 0.5, 3.0, ((0, 1024),)),
        "route_weight": jnp.clip(jnp.exp(math.log(1.0) - 2.306499 * jax.random.uniform(arg_keys[1], (TOKENS, TOPK), jnp.float32) ** steps_of(arg_keys[1], (TOKENS, TOPK), ((0, 1024),), -0.2, 0.2)), 0.099609375, 1.0).astype(jnp.bfloat16),
        "expert_ids": draw_expert_ids(jax.random.fold_in(arg_keys[8], 71), 0),
        "slot_ids": draw_slot_ids(jax.random.fold_in(arg_keys[8], 71), 0),
        "saved_pre": centred(arg_keys[4], (EXPERTS * HID_SPLIT, SLOTS, 2 * FF_DEV), 1.0, 6.0, ((0, 1024),)),
        "gate_proj": centred(arg_keys[5], (EXPERTS * HID_SPLIT, FF_DEV, D), D ** -0.5, 0.09375, ((0, 1024),)),
        "up_proj": centred(arg_keys[6], (EXPERTS * HID_SPLIT, FF_DEV, D), D ** -0.5, 0.09375, ((0, 1024),)),
        "down_proj": centred(arg_keys[7], (EXPERTS * HID_SPLIT, FF_DEV, D), FF ** -0.5, 0.15625, ((0, 1024),)),
    }


def reference(grad_out, route_weight, expert_ids, slot_ids, saved_pre, gate_proj, up_proj, down_proj):
    route_total = TOKENS * TOPK
    route_index = jnp.arange(route_total, dtype=jnp.int32)
    token_index = route_index // TOPK
    block_index = token_index // TOK_ROW
    place_index = expert_ids.reshape(-1).astype(jnp.int32) * SLOTS + block_index * CAP + slot_ids.reshape(-1).astype(jnp.int32)
    owners = jnp.full((EXPERTS * SLOTS,), route_total, jnp.int32).at[place_index].set(route_index)
    owners = owners.reshape(EXPERTS, SLOTS)
    weight_flat = route_weight.reshape(-1)
    pre_all = saved_pre.reshape(EXPERTS, HID_SPLIT, SLOTS, 2, FF_DEV)
    gate_all = gate_proj.reshape(EXPERTS, HID_SPLIT, FF_DEV, D)
    up_all = up_proj.reshape(EXPERTS, HID_SPLIT, FF_DEV, D)
    down_all = down_proj.reshape(EXPERTS, FF, D)

    def expert_step(carried, inputs):
        grad_sum, prob_sum = carried
        slot_owner, pre_local, gate_local, up_local, down_local = inputs
        filled = slot_owner < route_total
        safe_route = jnp.where(filled, slot_owner, 0).astype(jnp.int32)
        safe_token = (safe_route // TOPK).astype(jnp.int32)
        slot_rows = jnp.where(filled[:, None], grad_out[safe_token], jnp.zeros((), grad_out.dtype))
        slot_weight = jnp.where(filled, weight_flat[safe_route].astype(jnp.float32), jnp.zeros((), jnp.float32))[:, None]
        gate_pre = jnp.transpose(pre_local[:, :, 0, :], (1, 0, 2)).reshape(SLOTS, FF).astype(jnp.float32)
        up_pre = jnp.transpose(pre_local[:, :, 1, :], (1, 0, 2)).reshape(SLOTS, FF).astype(jnp.float32)
        sigmoid_gate = jax.nn.sigmoid(gate_pre)
        active = gate_pre * sigmoid_gate
        product = active * up_pre
        hidden = product.astype(jnp.bfloat16)
        weighted = (slot_weight * product).astype(jnp.bfloat16)
        back_proj = jnp.dot(slot_rows, down_local.T, preferred_element_type=jnp.float32)
        scaled = slot_weight * back_proj
        grad_gate = (scaled * up_pre * sigmoid_gate * (1.0 + gate_pre * (1.0 - sigmoid_gate))).astype(jnp.bfloat16)
        grad_up = (scaled * active).astype(jnp.bfloat16)
        gate_parts = jnp.einsum("shf,hfd->shd", grad_gate.reshape(SLOTS, HID_SPLIT, FF_DEV).astype(jnp.float32), gate_local.astype(jnp.float32))
        up_parts = jnp.einsum("shf,hfd->shd", grad_up.reshape(SLOTS, HID_SPLIT, FF_DEV).astype(jnp.float32), up_local.astype(jnp.float32))
        slice_parts = lax.optimization_barrier((gate_parts + up_parts).astype(jnp.bfloat16))
        route_grad = jnp.sum(slice_parts.astype(jnp.float32), axis=1)
        prob_parts = jnp.sum((hidden.astype(jnp.float32) * back_proj).reshape(SLOTS, HID_SPLIT, FF_DEV), axis=2)
        prob_parts = lax.optimization_barrier(prob_parts.astype(jnp.bfloat16))
        route_prob = jnp.sum(prob_parts.astype(jnp.float32), axis=1)
        grad_sum = grad_sum.at[jnp.where(filled, safe_token, TOKENS).astype(jnp.int32)].add(route_grad, mode="drop")
        prob_sum = prob_sum.at[jnp.where(filled, safe_route, route_total).astype(jnp.int32)].add(route_prob, mode="drop")
        down_grad = jnp.dot(weighted.T, slot_rows, preferred_element_type=jnp.float32).astype(jnp.bfloat16)
        return (grad_sum, prob_sum), down_grad

    start_carry = (jnp.zeros((TOKENS, D), jnp.float32), jnp.zeros((route_total,), jnp.float32))
    (grad_sum, prob_sum), down_grads = lax.scan(expert_step, start_carry, (owners, pre_all, gate_all, up_all, down_all))
    grad_tokens = grad_sum.astype(jnp.bfloat16)
    grad_weights = prob_sum.reshape(TOKENS, TOPK)
    grad_down = down_grads.reshape(EXPERTS * HID_SPLIT, FF_DEV, D)
    return (grad_tokens, grad_weights, grad_down)
```

```python
import jax
import jax.numpy as jnp
from jax import lax
from jax.experimental import pallas as pl
from jax.experimental.pallas import tpu as pltpu
from jax.sharding import PartitionSpec as P

MESH = pl.DeviceIdType.MESH
BF, F32 = jnp.bfloat16, jnp.float32
D, UNITS, TOPK, CAP = 4096, 96, 8, 30
SLOTS, PAD, BLOCKS = 240, 32, 8
ROWS = BLOCKS * PAD
EXT = 128
NX, NZ, NQ = 4, 32, 8
CHUNK = 1024
NCH = D // CHUNK
CUTS = [(0, EXT + CHUNK)] + [(EXT + f * CHUNK, CHUNK) for f in range(1, NCH)]
EXP_STEPS = [(dy, dc) for dy in (1, 3, 2, 0) for dc in (0, 1) if (dy, dc) != (0, 0)]


def dot(a, b, dims=((1,), (0,))):
    return lax.dot_general(a, b, (dims, ((), ())), preferred_element_type=F32)


def kernel(pay, pre, gate_hbm, up_hbm, down_hbm, tok_out, prob_out, down_out,
           abuf, bbuf, frows, g, st, s, ysend, yrecv, psend, precv, xsend, xrecv, acc,
           bsend, brecv, cbuf, arecv, arecv2, wgu, wdn,
           load_sem, a_s, a_r, b_s, b_r, x_s, x_r, y_s, y_r, p_s, p_r, u_s, u_r, v_s, v_r, w_s, w_r):
    ex, et = lax.axis_index("exp"), lax.axis_index("et")
    y, core = ex // 2, ex % 2
    x, z = et // NZ, et % NZ
    q = z // 4
    column = x * 2 + z // 16
    expert = ex * 8 + column

    def at_z(dz):
        return (ex, x * NZ + lax.rem(z + dz + NZ, NZ))

    def at_x(dx):
        return (ex, lax.rem(x + dx, NX) * NZ + z)

    def exp_of(step):
        dy, dc = step
        return lax.rem(y + dy, 4) * 2 + lax.rem(core + dc, 2)

    def slot(j):
        return lax.rem(q + j + NQ, NQ)

    def send(src, dst, ss, rs, device):
        copy = pltpu.make_async_remote_copy(
            src_ref=src, dst_ref=dst, send_sem=ss, recv_sem=rs, device_id=device, device_id_type=MESH)
        copy.start()
        return copy

    sent = []

    loads = [
        pltpu.make_async_copy(gate_hbm.at[0], wgu.at[pl.ds(0, UNITS)], load_sem.at[0]),
        pltpu.make_async_copy(up_hbm.at[0], wgu.at[pl.ds(128, UNITS)], load_sem.at[1]),
        pltpu.make_async_copy(down_hbm.at[0], wdn.at[pl.ds(0, UNITS)], load_sem.at[2]),
    ]
    for load in loads:
        load.start()

    barrier = pltpu.get_barrier_semaphore()
    partners = [at_z(d) for d in (1, -1, 2, -2, 4, -4, 8, -8)]
    partners += [at_x(d) for d in (1, 2, 3)]
    partners += [(exp_of(step), et) for step in EXP_STEPS]
    for device in partners:
        pl.semaphore_signal(barrier, inc=1, device_id=device, device_id_type=MESH)
    abuf[:, pl.ds(q, 1)] = pay[...].reshape(3, 1, 16, 128)
    pad = jnp.zeros((32, D), BF)
    wgu[pl.ds(UNITS, 32)] = pad
    wgu[pl.ds(128 + UNITS, 32)] = pad
    wdn[pl.ds(UNITS, 32)] = pad
    pl.semaphore_wait(barrier, len(partners))

    mine = abuf.at[:, pl.ds(q, 1)]
    first = [send(mine, mine, a_s.at[i], a_r.at[i], at_z(d)) for i, d in enumerate((4, -4, 8, -8))]
    for copy in first:
        copy.wait_recv()
    second = []
    for i, (j, d) in enumerate(((1, -8), (2, -8), (-1, 8))):
        part = abuf.at[:, pl.ds(slot(j), 1)]
        second.append(send(part, part, a_s.at[4 + i], a_r.at[4 + i], at_z(d)))
    for copy in second:
        copy.wait_recv()
    sent += first + second

    bbuf[0, 0:8] = abuf[0]
    bbuf[0, 8] = jnp.sum(abuf[2].astype(F32), axis=0).astype(BF)
    bbuf[0, 9:17] = abuf[1]
    low, high = pl.ds(0, 9), pl.ds(9, 8)
    near = [
        send(bbuf.at[0], bbuf.at[1], b_s.at[0], b_r.at[0], at_z(-1)),
        send(bbuf.at[0], bbuf.at[3], b_s.at[1], b_r.at[1], at_z(1)),
        send(bbuf.at[0, low], bbuf.at[2, low], b_s.at[2], b_r.at[2], at_z(-2)),
        send(bbuf.at[0, high], bbuf.at[2, high], b_s.at[3], b_r.at[3], at_z(2)),
    ]
    for copy in near:
        copy.wait_recv()
    sent += near

    for d in range(4):
        g[d * 8:d * 8 + 8, 0:EXT] = bbuf[d, 8, 0:8]
        for h in range(2):
            frows[(d * 2 + h) * 128:(d * 2 + h + 1) * 128] = (
                bbuf[d, h * 9:h * 9 + 8].astype(F32).reshape(128, 128))
    gathers = []
    for f, (start, width) in enumerate(CUTS):
        h = f // 2
        for i in range((f % 2) * 8, (f % 2) * 8 + 8):
            row = jnp.concatenate(
                [frows[pl.ds((d * 2 + h) * 128 + i, 8, stride=16), :] for d in range(4)], axis=0)
            col = EXT + (h * 16 + i) * 128
            g[0:32, col:col + 128] = row.astype(BF)
        cols = pl.ds(start, width)
        gathers.append([
            send(g.at[pl.ds(0, 32), cols], g.at[pl.ds((4 - dx) * 32, 32), cols],
                 x_s.at[dx - 1, f], x_r.at[dx - 1, f], at_x(dx))
            for dx in (1, 2, 3)])

    mine_rows = pl.ds(pl.multiple_of(ex * PAD, PAD), PAD)
    dispatch = []
    for f, (start, width) in enumerate(CUTS):
        cols = pl.ds(start, width)
        for copy in gathers[f]:
            copy.wait_recv()
        if f == 0:
            ext = g[:, 0:EXT].astype(F32)
            code = ext * 32.0 + pltpu.roll(ext, EXT - TOPK, 1)
            lane = lax.broadcasted_iota(jnp.int32, (128, ROWS), 1)
            target = ((lane // PAD) * 256 + lane % PAD + column * PAD).astype(F32)
            hit = jnp.zeros((128, ROWS), F32)
            for k in range(TOPK):
                hit = hit + jnp.where(code[:, k:k + 1] == target, 1.0, 0.0)
            st[...] = hit.astype(BF)
            s[...] = jnp.transpose(hit).astype(BF)
        ysend[:, start:start + width] = dot(s[...], g[:, start:start + width]).astype(BF)
        copies = []
        for j, step in enumerate(EXP_STEPS):
            to = exp_of(step)
            rows = pl.ds(pl.multiple_of(to * PAD, PAD), PAD)
            copies.append(send(ysend.at[rows, cols], yrecv.at[mine_rows, cols],
                               y_s.at[j, f], y_r.at[j, f], (to, et)))
        yrecv[mine_rows, start:start + width] = ysend[mine_rows, start:start + width]
        dispatch.append(copies)

    for load in loads:
        load.wait()
    slot_row = lax.broadcasted_iota(jnp.int32, (ROWS, SLOTS), 0)
    slot_col = lax.broadcasted_iota(jnp.int32, (ROWS, SLOTS), 1)
    place = (slot_row // PAD) * CAP + slot_row % PAD
    spread = jnp.where((place == slot_col) & (slot_row % PAD < CAP), 1.0, 0.0).astype(BF)
    pre_rows = dot(spread, pre[...]).astype(BF)
    unit_row = lax.broadcasted_iota(jnp.int32, (2 * UNITS, 128), 0)
    unit_col = lax.broadcasted_iota(jnp.int32, (2 * UNITS, 128), 1)
    pick_gate = jnp.where((unit_row == unit_col) & (unit_col < UNITS), 1.0, 0.0).astype(BF)
    pick_up = jnp.where((unit_row == unit_col + UNITS) & (unit_col < UNITS), 1.0, 0.0).astype(BF)
    gate_pre = dot(pre_rows, pick_gate)
    up_pre = dot(pre_rows, pick_up)
    sig = jax.nn.sigmoid(gate_pre)
    active = gate_pre * sig
    product = active * up_pre
    hidden = product.astype(BF).astype(F32)
    gate_factor = up_pre * sig * (1.0 + gate_pre * (1.0 - sig))

    back = jnp.zeros((ROWS, 128), F32)
    for f, (start, width) in enumerate(CUTS):
        for copy in dispatch[f]:
            copy.wait_recv()
        back = back + dot(yrecv[:, EXT + f * CHUNK:EXT + (f + 1) * CHUNK],
                          wdn[:, f * CHUNK:(f + 1) * CHUNK], ((1,), (1,)))
        sent += dispatch[f] + gathers[f]

    ext = yrecv[:, 0:EXT].astype(F32)
    lane = lax.broadcasted_iota(jnp.int32, (ROWS, EXT), 1)
    named = (lane < TOPK) & (ext.astype(jnp.int32) == expert)
    weight = jnp.sum(jnp.where(named, pltpu.roll(ext, EXT - 2 * TOPK, 1), 0.0), axis=1, keepdims=True)
    scaled = weight * back
    grads = jnp.concatenate([scaled * gate_factor, scaled * active], axis=1).astype(BF)
    part_prob = jnp.sum(hidden * back, axis=1, keepdims=True)
    psend[:, 0:EXT] = jnp.where(named, part_prob, 0.0).astype(BF)
    weighted = jnp.transpose(weight * product).astype(BF)

    combine = []
    for f, (start, width) in enumerate(CUTS):
        cols = pl.ds(start, width)
        psend[:, EXT + f * CHUNK:EXT + (f + 1) * CHUNK] = dot(
            grads, wgu[:, f * CHUNK:(f + 1) * CHUNK]).astype(BF)
        copies = []
        for j, step in enumerate(EXP_STEPS):
            to = exp_of(step)
            rows = pl.ds(pl.multiple_of(to * PAD, PAD), PAD)
            copies.append(send(psend.at[rows, cols], precv.at[mine_rows, cols],
                               p_s.at[j, f], p_r.at[j, f], (to, et)))
        precv[mine_rows, start:start + width] = psend[mine_rows, start:start + width]
        combine.append(copies)

    for f in range(NCH):
        down_out[:, f * CHUNK:(f + 1) * CHUNK] = dot(
            weighted, yrecv[:, EXT + f * CHUNK:EXT + (f + 1) * CHUNK])[0:UNITS].astype(BF)

    reduces = []
    for f, (start, width) in enumerate(CUTS):
        cols = pl.ds(start, width)
        for copy in combine[f]:
            copy.wait_recv()
        sent += combine[f]
        dense = dot(st[...], precv[:, start:start + width])
        acc[:, start:start + width] = dense[0:32]
        xsend[:, start:start + width] = dense[32:128].astype(BF)
        reduces.append([
            send(xsend.at[pl.ds((dx - 1) * 32, 32), cols], xrecv.at[dx - 1, :, cols],
                 u_s.at[dx - 1, f], u_r.at[dx - 1, f], at_x(dx))
            for dx in (1, 2, 3)])
    for f, (start, width) in enumerate(CUTS):
        for copy in reduces[f]:
            copy.wait_recv()
        sent += reduces[f]
        total = acc[:, start:start + width]
        for i in range(3):
            total = total + xrecv[i, :, start:start + width].astype(F32)
        if f == 0:
            ext_total = total[:, 0:EXT]
            total = total[:, EXT:]
        h = f // 2
        for i in range(8):
            for d in range(4):
                frows[pl.ds((d * 2 + h) * 128 + (f % 2) * 8 + i, 8, stride=16), :] = (
                    total[d * 8:d * 8 + 8, i * 128:(i + 1) * 128])

    for d in range(1, 4):
        for h in range(2):
            bsend[d - 1, h * 9:h * 9 + 8] = (
                frows[(d * 2 + h) * 128:(d * 2 + h + 1) * 128].reshape(8, 16, 128).astype(BF))
        bsend[d - 1, 8] = jnp.concatenate(
            [ext_total[d * 8:d * 8 + 8], jnp.zeros((8, 128), F32)], axis=0).astype(BF)
    near = [
        send(bsend.at[0], brecv.at[0], v_s.at[0], v_r.at[0], at_z(1)),
        send(bsend.at[2], brecv.at[1], v_s.at[1], v_r.at[1], at_z(-1)),
        send(bsend.at[1, low], brecv.at[2, low], v_s.at[2], v_r.at[2], at_z(2)),
        send(bsend.at[1, high], brecv.at[2, high], v_s.at[3], v_r.at[3], at_z(-2)),
    ]
    for copy in near:
        copy.wait_recv()
    sent += near
    for h in range(2):
        total = frows[h * 128:(h + 1) * 128].reshape(8, 16, 128)
        for i in range(3):
            total = total + brecv[i, h * 9:h * 9 + 8].astype(F32)
        cbuf[h] = total
    total = jnp.concatenate([ext_total[0:8], jnp.zeros((8, 128), F32)], axis=0)
    for i in range(3):
        total = total + brecv[i, 8].astype(F32)
    for j in range(8):
        cbuf[2, j] = total

    for j in range(8):
        arecv2[:, j] = cbuf[:, j].astype(BF)
    third = []
    for i, (j, d) in enumerate(((3, 8), (4, 8), (-3, -8))):
        third.append(send(arecv2.at[:, pl.ds(slot(j), 1)], arecv.at[i], w_s.at[i], w_r.at[i], at_z(d)))
    for copy in third:
        copy.wait_recv()
    for i, j in enumerate((1, 2, -1)):
        part = cbuf[:, pl.ds(slot(j), 1)] + arecv[i].astype(F32)
        arecv2[:, pl.ds(slot(j), 1)] = part.astype(BF)
    fourth = []
    for i, (j, d) in enumerate(((1, 4), (-1, -4), (2, 8), (-2, -8))):
        fourth.append(send(arecv2.at[:, pl.ds(slot(j), 1)], arecv.at[3 + i],
                           w_s.at[3 + i], w_r.at[3 + i], at_z(d)))
    for copy in fourth:
        copy.wait_recv()
    sent += third + fourth
    total = cbuf[:, pl.ds(q, 1)]
    for i in range(4):
        total = total + arecv[3 + i].astype(F32)
    total = total.reshape(3, 16, 128)
    tok_out[...] = total[0:2].astype(BF)
    prob_out[...] = total[2]
    for copy in sent:
        copy.wait_send()


def body(grad_out, route_weight, expert_ids, slot_ids, saved_pre, gate_proj, up_proj, down_proj):
    q = lax.axis_index("et") % NZ // 4
    extra = jnp.concatenate(
        [expert_ids.astype(BF), slot_ids.astype(BF), route_weight, jnp.zeros((1, EXT - 3 * TOPK), BF)], axis=1)
    extra = jnp.where(jnp.arange(16)[:, None] == q, extra, jnp.zeros((), BF))
    pay = jnp.concatenate([grad_out.reshape(2, 16, 128), extra[None]], axis=0)
    vmem = pl.BlockSpec(memory_space=pltpu.VMEM)
    hbm = pl.BlockSpec(memory_space=pl.ANY)
    wide = EXT + D
    dma = lambda *shape: pltpu.SemaphoreType.DMA(shape)
    tokens, probs, down_grad = pl.pallas_call(
        kernel,
        out_shape=(
            jax.ShapeDtypeStruct((2, 16, 128), BF),
            jax.ShapeDtypeStruct((16, 128), F32),
            jax.ShapeDtypeStruct((UNITS, D), BF),
        ),
        in_specs=[vmem, vmem, hbm, hbm, hbm],
        out_specs=(vmem, vmem, vmem),
        scratch_shapes=[
            pltpu.VMEM((3, 8, 16, 128), BF),
            pltpu.VMEM((4, 17, 16, 128), BF),
            pltpu.VMEM((1024, 128), F32),
            pltpu.VMEM((128, wide), BF),
            pltpu.VMEM((128, ROWS), BF),
            pltpu.VMEM((ROWS, 128), BF),
            pltpu.VMEM((ROWS, wide), BF),
            pltpu.VMEM((ROWS, wide), BF),
            pltpu.VMEM((ROWS, wide), BF),
            pltpu.VMEM((ROWS, wide), BF),
            pltpu.VMEM((96, wide), BF),
            pltpu.VMEM((3, 32, wide), BF),
            pltpu.VMEM((32, wide), F32),
            pltpu.VMEM((3, 17, 16, 128), BF),
            pltpu.VMEM((3, 17, 16, 128), BF),
            pltpu.VMEM((3, 8, 16, 128), F32),
            pltpu.VMEM((7, 3, 1, 16, 128), BF),
            pltpu.VMEM((3, 8, 16, 128), BF),
            pltpu.VMEM((256, D), BF),
            pltpu.VMEM((128, D), BF),
            dma(3), dma(7), dma(7), dma(4), dma(4), dma(3, NCH), dma(3, NCH), dma(7, NCH), dma(7, NCH),
            dma(7, NCH), dma(7, NCH), dma(3, NCH), dma(3, NCH), dma(4), dma(4), dma(7), dma(7),
        ],
        compiler_params=pltpu.CompilerParams(
            collective_id=0, has_side_effects=True, vmem_limit_bytes=50 * 2**20),
    )(pay, saved_pre[0], gate_proj, up_proj, down_proj)
    return tokens.reshape(1, D), lax.dynamic_slice(probs, (q, 0), (1, TOPK)), down_grad[None]


def solution(mesh):
    rows, blocks = P(("exp", "et"), None), P(("exp", "et"), None, None)
    return jax.shard_map(
        body, mesh=mesh, in_specs=(rows, rows, rows, rows, blocks, blocks, blocks, blocks),
        out_specs=(rows, rows, blocks), check_vma=False)
```

```python
import jax
import jax.numpy as jnp
from jax import lax
from jax.experimental import pallas as pl
from jax.experimental.pallas import tpu as pltpu
from jax.sharding import PartitionSpec as P

MESH = pl.DeviceIdType.MESH
BF, F32 = jnp.bfloat16, jnp.float32
D, UNITS, TOPK, CAP = 4096, 96, 8, 30
SLOTS, PAD, BLOCKS = 240, 32, 8
ROWS = BLOCKS * PAD
EXT = 128
NX, NZ, NQ = 4, 32, 8
OWN, BOTH = 8, 16
WO, WB = OWN * 128, BOTH * 128
WIDE = EXT + WO + WB
CUTS = [(0, EXT + WO // 2), (EXT + WO // 2, WO // 2), (EXT + WO, WB // 2), (EXT + WO + WB // 2, WB // 2)]
NCH = len(CUTS)
BACK_ORDER = (2, 3, 0, 1)


def features(f):
    start, width = CUTS[f]
    return (EXT, start + width) if f == 0 else (start, start + width)


EXP_STEPS = [(dy, dc) for dy in (1, 3, 2, 0) for dc in (0, 1) if (dy, dc) != (0, 0)]


def dot(a, b, dims=((1,), (0,))):
    return lax.dot_general(a, b, (dims, ((), ())), preferred_element_type=F32)


def kernel(grad_in, weights_in, ids_in, places_in, pre_in, gate_hbm, up_hbm, down_hbm, tok_out, prob_out, down_out,
           grad, weights, ids, places, pre, tok, prob, gdown,
           abuf, bbuf, frows, g, st, s, ysend, yrecv, psend, precv, xsend, xrecv, acc,
           bsend, brecv, cbuf, arecv, arecv2, wgu, wdn, zsend, zrecv,
           load_sem, a_s, a_r, b_s, b_r, x_s, x_r, y_s, y_r, p_s, p_r, u_s, u_r, v_s, v_r, w_s, w_r, f_s, f_r, z_s, z_r):
    ex, et = lax.axis_index("exp"), lax.axis_index("et")
    y, core = ex // 2, ex % 2
    x, z = et // NZ, et % NZ
    q = z // 4
    odd = z % 2
    own_at = pl.multiple_of(WB + odd * WO, WO)
    other_at = pl.multiple_of(WB + (1 - odd) * WO, WO)
    column = x * 2 + z // 16
    expert = ex * 8 + column

    def at_z(dz):
        return (ex, x * NZ + lax.rem(z + dz + NZ, NZ))

    def at_x(dx):
        return (ex, lax.rem(x + dx, NX) * NZ + z)

    def exp_of(step):
        dy, dc = step
        return lax.rem(y + dy, 4) * 2 + lax.rem(core + dc, 2)

    def slot(j):
        return lax.rem(q + j + NQ, NQ)

    def send(src, dst, ss, rs, device):
        copy = pltpu.make_async_remote_copy(
            src_ref=src, dst_ref=dst, send_sem=ss, recv_sem=rs, device_id=device, device_id_type=MESH)
        copy.start()
        return copy

    sent = []

    barrier = pltpu.get_barrier_semaphore()
    partners = [at_z(d) for d in (8, -8, 4, -4, 2, -2, 1, -1)]
    partners += [at_x(d) for d in (1, 2, 3)]
    partners += [(exp_of(step), et) for step in EXP_STEPS]
    for device in partners:
        pl.semaphore_signal(barrier, inc=1, device_id=device, device_id_type=MESH)

    early = [pltpu.make_async_copy(src, dst, load_sem.at[i]) for i, (src, dst) in enumerate(
        ((grad_in, grad), (weights_in, weights), (ids_in, ids), (places_in, places)))]
    loads = [pltpu.make_async_copy(pre_in, pre, load_sem.at[4])]
    for i, (src, dst, row) in enumerate(((gate_hbm, wgu, 0), (up_hbm, wgu, 128), (down_hbm, wdn, 0))):
        for j, (at, to, width) in enumerate(((own_at, 0, WO), (0, WO, WB), (other_at, WO + WB, WO))):
            loads.append(pltpu.make_async_copy(
                src.at[0, :, pl.ds(at, width)], dst.at[pl.ds(row, UNITS), pl.ds(to, width)],
                load_sem.at[8 + i * 3 + j]))
    for load in early + loads:
        load.start()
    for load in early:
        load.wait()
    for i in range(D // 128):
        frows[i:i + 1, :] = grad[0:1, i * 128:(i + 1) * 128].astype(F32)
    abuf[0:2, pl.ds(q, 1)] = frows[0:32].reshape(2, 1, 16, 128).astype(BF)
    extra = jnp.concatenate(
        [ids[...].astype(F32), places[...].astype(F32), weights[...].astype(F32),
         jnp.zeros((1, EXT - 3 * TOPK), F32)], axis=1)
    own_row = lax.broadcasted_iota(jnp.int32, (16, 128), 0) == q
    abuf[2:3, pl.ds(q, 1)] = jnp.where(own_row, extra, 0.0).reshape(1, 1, 16, 128).astype(BF)
    pad = jnp.zeros((32, D), BF)
    wgu[pl.ds(UNITS, 32)] = pad
    wgu[pl.ds(128 + UNITS, 32)] = pad
    wdn[pl.ds(UNITS, 32)] = pad
    pl.semaphore_wait(barrier, len(partners))

    mine = abuf.at[:, pl.ds(q, 1)]
    first = [send(mine, mine, a_s.at[i], a_r.at[i], at_z(d)) for i, d in enumerate((4, -4, 8, -8))]
    for copy in first:
        copy.wait_recv()
    second = []
    for i, (j, d) in enumerate(((1, -8), (2, -8), (-1, 8))):
        part = abuf.at[:, pl.ds(slot(j), 1)]
        second.append(send(part, part, a_s.at[4 + i], a_r.at[4 + i], at_z(d)))
    for copy in second:
        copy.wait_recv()
    sent += first + second

    bbuf[0, 0:8] = abuf[0]
    bbuf[0, 8] = jnp.sum(abuf[2].astype(F32), axis=0).astype(BF)
    bbuf[0, 9:17] = abuf[1]
    low, high = pl.ds(0, 9), pl.ds(9, 8)
    near = [
        send(bbuf.at[0], bbuf.at[1], b_s.at[0], b_r.at[0], at_z(-1)),
        send(bbuf.at[0], bbuf.at[3], b_s.at[1], b_r.at[1], at_z(1)),
        send(bbuf.at[0, low], bbuf.at[2, low], b_s.at[2], b_r.at[2], at_z(-2)),
        send(bbuf.at[0, high], bbuf.at[2, high], b_s.at[3], b_r.at[3], at_z(2)),
    ]
    for copy in near:
        copy.wait_recv()
    sent += near

    for d in range(4):
        g[d * 8:d * 8 + 8, 0:EXT] = bbuf[d, 8, 0:8]
        for h in range(2):
            frows[(d * 2 + h) * 128:(d * 2 + h + 1) * 128] = (
                bbuf[d, h * 9:h * 9 + 8].astype(F32).reshape(128, 128))
    gathers = []

    def unit(u):
        return jnp.concatenate(
            [frows[pl.ds((d * 2 + u // 16) * 128 + u % 16, 8, stride=16), :] for d in range(4)], axis=0)

    for f, (start, width) in enumerate(CUTS):
        begin, end = features(f)
        for col in range(begin, end, 128):
            v = (col - EXT) // 128
            if v < OWN:
                row = jnp.where(odd == 0, unit(BOTH + v), unit(BOTH + OWN + v))
            else:
                row = unit(v - OWN)
            g[0:32, col:col + 128] = row.astype(BF)
        cols = pl.ds(start, width)
        gathers.append([
            send(g.at[pl.ds(0, 32), cols], g.at[pl.ds((4 - dx) * 32, 32), cols],
                 x_s.at[dx - 1, f], x_r.at[dx - 1, f], at_x(dx))
            for dx in (1, 2, 3)])

    mine_rows = pl.ds(pl.multiple_of(ex * PAD, PAD), PAD)
    dispatch = []
    for f, (start, width) in enumerate(CUTS):
        cols = pl.ds(start, width)
        for copy in gathers[f]:
            copy.wait_recv()
        if f == 0:
            ext = g[:, 0:EXT].astype(F32)
            code = ext * 32.0 + pltpu.roll(ext, EXT - TOPK, 1)
            lane = lax.broadcasted_iota(jnp.int32, (128, ROWS), 1)
            target = ((lane // PAD) * 256 + lane % PAD + column * PAD).astype(F32)
            hit = jnp.zeros((128, ROWS), F32)
            for k in range(TOPK):
                hit = hit + jnp.where(code[:, k:k + 1] == target, 1.0, 0.0)
            st[...] = hit.astype(BF)
            s[...] = jnp.transpose(hit).astype(BF)
        ysend[:, start:start + width] = dot(s[...], g[:, start:start + width]).astype(BF)
        copies = []
        for j, step in enumerate(EXP_STEPS):
            to = exp_of(step)
            rows = pl.ds(pl.multiple_of(to * PAD, PAD), PAD)
            copies.append(send(ysend.at[rows, cols], yrecv.at[mine_rows, cols],
                               y_s.at[j, f], y_r.at[j, f], (to, et)))
        yrecv[mine_rows, start:start + width] = ysend[mine_rows, start:start + width]
        dispatch.append(copies)

    for load in loads:
        load.wait()
    slot_row = lax.broadcasted_iota(jnp.int32, (ROWS, SLOTS), 0)
    slot_col = lax.broadcasted_iota(jnp.int32, (ROWS, SLOTS), 1)
    place = (slot_row // PAD) * CAP + slot_row % PAD
    spread = jnp.where((place == slot_col) & (slot_row % PAD < CAP), 1.0, 0.0).astype(BF)
    pre_rows = dot(spread, pre[0], ((1,), (1,))).astype(BF)
    unit_row = lax.broadcasted_iota(jnp.int32, (2 * UNITS, 128), 0)
    unit_col = lax.broadcasted_iota(jnp.int32, (2 * UNITS, 128), 1)
    pick_gate = jnp.where((unit_row == unit_col) & (unit_col < UNITS), 1.0, 0.0).astype(BF)
    pick_up = jnp.where((unit_row == unit_col + UNITS) & (unit_col < UNITS), 1.0, 0.0).astype(BF)
    gate_pre = dot(pre_rows, pick_gate)
    up_pre = dot(pre_rows, pick_up)
    sig = jax.nn.sigmoid(gate_pre)
    active = gate_pre * sig
    product = active * up_pre
    hidden = product.astype(BF).astype(F32)
    gate_factor = up_pre * sig * (1.0 + gate_pre * (1.0 - sig))

    pair = at_z(1 - 2 * odd)
    half = WO // 2
    forwards = []
    back = jnp.zeros((ROWS, 128), F32)
    for f in range(NCH):
        begin, end = features(f)
        for copy in dispatch[f]:
            copy.wait_recv()
        if f < 2:
            forwards.append(send(
                yrecv.at[:, pl.ds(begin, half)], yrecv.at[:, pl.ds(WIDE + f * half, half)],
                f_s.at[f], f_r.at[f], pair))
        back = back + dot(yrecv[:, begin:end], wdn[:, begin - EXT:end - EXT], ((1,), (1,)))
        sent += dispatch[f] + gathers[f]
    for f in range(2):
        forwards[f].wait_recv()
        begin = WIDE + f * half
        back = back + dot(yrecv[:, begin:begin + half], wdn[:, begin - EXT:begin - EXT + half], ((1,), (1,)))
    sent += forwards

    ext = yrecv[:, 0:EXT].astype(F32)
    lane = lax.broadcasted_iota(jnp.int32, (ROWS, EXT), 1)
    named = (lane < TOPK) & (ext.astype(jnp.int32) == expert)
    weight = jnp.sum(jnp.where(named, pltpu.roll(ext, EXT - 2 * TOPK, 1), 0.0), axis=1, keepdims=True)
    scaled = weight * back
    grads = jnp.concatenate([scaled * gate_factor, scaled * active], axis=1).astype(BF)
    part_prob = jnp.sum(hidden * back, axis=1, keepdims=True)
    psend[:, 0:EXT] = jnp.where(named, part_prob, 0.0).astype(BF)
    weighted = jnp.transpose(weight * product).astype(BF)

    swaps = []
    for f in range(2):
        begin = WO + WB + f * half
        zsend[:, f * half:(f + 1) * half] = dot(grads, wgu[:, begin:begin + half]).astype(BF)
        part = pl.ds(f * half, half)
        swaps.append(send(zsend.at[:, part], zrecv.at[:, part], z_s.at[f], z_r.at[f], pair))
    combine = [None] * NCH
    for f in BACK_ORDER:
        start, width = CUTS[f]
        begin, end = features(f)
        cols = pl.ds(start, width)
        part = dot(grads, wgu[:, begin - EXT:end - EXT])
        if f < 2:
            swaps[f].wait_recv()
            part = part + zrecv[:, f * half:(f + 1) * half].astype(F32)
        psend[:, begin:end] = part.astype(BF)
        copies = []
        for j, step in enumerate(EXP_STEPS):
            to = exp_of(step)
            rows = pl.ds(pl.multiple_of(to * PAD, PAD), PAD)
            copies.append(send(psend.at[rows, cols], precv.at[mine_rows, cols],
                               p_s.at[j, f], p_r.at[j, f], (to, et)))
        precv[mine_rows, start:start + width] = psend[mine_rows, start:start + width]
        combine[f] = copies
        if f == 3:
            for at, begin, width in ((0, EXT + WO, WB), (own_at, EXT, WO), (other_at, WIDE, WO)):
                gdown[:, pl.ds(at, width)] = dot(weighted, yrecv[:, begin:begin + width])[0:UNITS].astype(BF)
    sent += swaps
    stores = [pltpu.make_async_copy(gdown, down_out, load_sem.at[5])]
    stores[0].start()

    reduces = [None] * NCH
    for f in BACK_ORDER:
        start, width = CUTS[f]
        cols = pl.ds(start, width)
        for copy in combine[f]:
            copy.wait_recv()
        sent += combine[f]
        dense = dot(st[...], precv[:, start:start + width])
        acc[:, start:start + width] = dense[0:32]
        xsend[:, start:start + width] = dense[32:128].astype(BF)
        reduces[f] = [
            send(xsend.at[pl.ds((dx - 1) * 32, 32), cols], xrecv.at[dx - 1, :, cols],
                 u_s.at[dx - 1, f], u_r.at[dx - 1, f], at_x(dx))
            for dx in (1, 2, 3)]

    def put(u, rows):
        for d in range(4):
            frows[pl.ds((d * 2 + u // 16) * 128 + u % 16, 8, stride=16), :] = rows[d * 8:d * 8 + 8]

    for f in BACK_ORDER:
        start, width = CUTS[f]
        begin, end = features(f)
        for copy in reduces[f]:
            copy.wait_recv()
        sent += reduces[f]
        total = acc[:, start:start + width]
        for i in range(3):
            total = total + xrecv[i, :, start:start + width].astype(F32)
        if f == 0:
            ext_total = total[:, 0:EXT]
        for col in range(begin, end, 128):
            v = (col - EXT) // 128
            rows = total[:, col - start:col - start + 128]
            if v < OWN:
                put(BOTH + v, jnp.where(odd == 0, rows, 0.0))
                put(BOTH + OWN + v, jnp.where(odd == 0, 0.0, rows))
            else:
                put(v - OWN, rows)

    for d in range(1, 4):
        for h in range(2):
            bsend[d - 1, h * 9:h * 9 + 8] = (
                frows[(d * 2 + h) * 128:(d * 2 + h + 1) * 128].reshape(8, 16, 128).astype(BF))
        bsend[d - 1, 8] = jnp.concatenate(
            [ext_total[d * 8:d * 8 + 8], jnp.zeros((8, 128), F32)], axis=0).astype(BF)
    near = [
        send(bsend.at[0], brecv.at[0], v_s.at[0], v_r.at[0], at_z(1)),
        send(bsend.at[2], brecv.at[1], v_s.at[1], v_r.at[1], at_z(-1)),
        send(bsend.at[1, low], brecv.at[2, low], v_s.at[2], v_r.at[2], at_z(2)),
        send(bsend.at[1, high], brecv.at[2, high], v_s.at[3], v_r.at[3], at_z(-2)),
    ]
    for copy in near:
        copy.wait_recv()
    sent += near
    for h in range(2):
        total = frows[h * 128:(h + 1) * 128].reshape(8, 16, 128)
        for i in range(3):
            total = total + brecv[i, h * 9:h * 9 + 8].astype(F32)
        cbuf[h] = total
    total = jnp.concatenate([ext_total[0:8], jnp.zeros((8, 128), F32)], axis=0)
    for i in range(3):
        total = total + brecv[i, 8].astype(F32)
    for j in range(8):
        cbuf[2, j] = total

    for j in range(8):
        arecv2[:, j] = cbuf[:, j].astype(BF)
    third = []
    for i, (j, d) in enumerate(((3, 8), (4, 8), (-3, -8))):
        third.append(send(arecv2.at[:, pl.ds(slot(j), 1)], arecv.at[i], w_s.at[i], w_r.at[i], at_z(d)))
    for copy in third:
        copy.wait_recv()
    for i, j in enumerate((1, 2, -1)):
        part = cbuf[:, pl.ds(slot(j), 1)] + arecv[i].astype(F32)
        arecv2[:, pl.ds(slot(j), 1)] = part.astype(BF)
    fourth = []
    for i, (j, d) in enumerate(((1, 4), (-1, -4), (2, 8), (-2, -8))):
        fourth.append(send(arecv2.at[:, pl.ds(slot(j), 1)], arecv.at[3 + i],
                           w_s.at[3 + i], w_r.at[3 + i], at_z(d)))
    for copy in fourth:
        copy.wait_recv()
    sent += third + fourth
    total = cbuf[:, pl.ds(q, 1)]
    for i in range(4):
        total = total + arecv[3 + i].astype(F32)
    total = total.reshape(3, 16, 128)
    frows[0:32] = total[0:2].reshape(32, 128)
    for i in range(D // 128):
        tok[0:1, i * 128:(i + 1) * 128] = frows[i:i + 1, :].astype(BF)
    prob[...] = jnp.sum(jnp.where(own_row, total[2], 0.0), axis=0, keepdims=True)[:, 0:TOPK]
    for i, (src, dst) in enumerate(((tok, tok_out), (prob, prob_out))):
        stores.append(pltpu.make_async_copy(src, dst, load_sem.at[6 + i]))
        stores[-1].start()
    for copy in sent:
        copy.wait_send()
    for store in stores:
        store.wait()


def deliver(tok, prob, down, tok_out, prob_out, down_out, tok_buf, prob_buf, down_buf, in_sem, out_sem):
    parts = [(tok, tok_buf, tok_out), (prob, prob_buf, prob_out)]
    for i in range(0, UNITS, 32):
        rows = pl.ds(i, 32)
        parts.append((down.at[rows], down_buf.at[rows], down_out.at[rows]))
    ins = [pltpu.make_async_copy(src, buf, in_sem.at[i]) for i, (src, buf, _) in enumerate(parts)]
    outs = [pltpu.make_async_copy(buf, dst, out_sem.at[i]) for i, (_, buf, dst) in enumerate(parts)]
    for copy in ins:
        copy.start()
    for copy, onward in zip(ins, outs):
        copy.wait()
        onward.start()
    for copy in outs:
        copy.wait()


def body(grad_out, route_weight, expert_ids, slot_ids, saved_pre, gate_proj, up_proj, down_proj):
    hbm = pl.BlockSpec(memory_space=pl.ANY)
    dma = lambda *shape: pltpu.SemaphoreType.DMA(shape)
    outs = (
        jax.ShapeDtypeStruct((1, D), BF),
        jax.ShapeDtypeStruct((1, TOPK), F32),
        jax.ShapeDtypeStruct((UNITS, D), BF),
    )
    results = pl.pallas_call(
        kernel,
        out_shape=outs,
        in_specs=[hbm] * 8,
        out_specs=(hbm,) * 3,
        scratch_shapes=[
            pltpu.VMEM((1, D), BF),
            pltpu.VMEM((1, TOPK), BF),
            pltpu.VMEM((1, TOPK), jnp.int32),
            pltpu.VMEM((1, TOPK), jnp.int32),
            pltpu.VMEM((1, 2 * UNITS, SLOTS), BF),
            pltpu.VMEM((1, D), BF),
            pltpu.VMEM((1, TOPK), F32),
            pltpu.VMEM((UNITS, D), BF),
            pltpu.VMEM((3, 8, 16, 128), BF),
            pltpu.VMEM((4, 17, 16, 128), BF),
            pltpu.VMEM((1024, 128), F32),
            pltpu.VMEM((128, WIDE), BF),
            pltpu.VMEM((128, ROWS), BF),
            pltpu.VMEM((ROWS, 128), BF),
            pltpu.VMEM((ROWS, WIDE), BF),
            pltpu.VMEM((ROWS, EXT + D), BF),
            pltpu.VMEM((ROWS, WIDE), BF),
            pltpu.VMEM((ROWS, WIDE), BF),
            pltpu.VMEM((96, WIDE), BF),
            pltpu.VMEM((3, 32, WIDE), BF),
            pltpu.VMEM((32, WIDE), F32),
            pltpu.VMEM((3, 17, 16, 128), BF),
            pltpu.VMEM((3, 17, 16, 128), BF),
            pltpu.VMEM((3, 8, 16, 128), F32),
            pltpu.VMEM((7, 3, 1, 16, 128), BF),
            pltpu.VMEM((3, 8, 16, 128), BF),
            pltpu.VMEM((256, D), BF),
            pltpu.VMEM((128, D), BF),
            pltpu.VMEM((ROWS, WO), BF),
            pltpu.VMEM((ROWS, WO), BF),
            dma(17), dma(7), dma(7), dma(4), dma(4), dma(3, NCH), dma(3, NCH), dma(7, NCH), dma(7, NCH),
            dma(7, NCH), dma(7, NCH), dma(3, NCH), dma(3, NCH), dma(4), dma(4), dma(7), dma(7),
            dma(2), dma(2), dma(2), dma(2),
        ],
        compiler_params=pltpu.CompilerParams(
            collective_id=0, has_side_effects=True, vmem_limit_bytes=60 * 2**20),
    )(grad_out, route_weight, expert_ids, slot_ids, jnp.swapaxes(saved_pre, 1, 2), gate_proj, up_proj, down_proj)
    tokens, probs, down_grad = pl.pallas_call(
        deliver,
        out_shape=outs,
        in_specs=[hbm] * 3,
        out_specs=(hbm,) * 3,
        scratch_shapes=[
            pltpu.VMEM((1, D), BF), pltpu.VMEM((1, TOPK), F32), pltpu.VMEM((UNITS, D), BF), dma(5), dma(5)],
    )(*results)
    return tokens, probs, down_grad[None]


def solution(mesh):
    rows, blocks = P(("exp", "et"), None), P(("exp", "et"), None, None)
    return jax.shard_map(
        body, mesh=mesh, in_specs=(rows, rows, rows, rows, blocks, blocks, blocks, blocks),
        out_specs=(rows, rows, blocks), check_vma=False)
```

```python
import jax
import jax.numpy as jnp
from jax import lax
from jax.experimental import pallas as pl
from jax.experimental.pallas import tpu as pltpu
from jax.sharding import PartitionSpec as P

MESH = pl.DeviceIdType.MESH
BF, F32 = jnp.bfloat16, jnp.float32
D, UNITS, TOPK, CAP = 4096, 96, 8, 30
SLOTS, PAD, BLOCKS = 240, 32, 8
ROWS = BLOCKS * PAD
EXT = 128
NX, NZ = 4, 32
OWN, BOTH = 8, 16
WO, WB = OWN * 128, BOTH * 128
WIDE = EXT + WO + WB
CUTS = [(0, EXT + WO // 2), (EXT + WO // 2, WO // 2), (EXT + WO, WB // 2), (EXT + WO + WB // 2, WB // 2)]
NCH = len(CUTS)
BACK_ORDER = (2, 3, 0, 1)


def features(f):
    start, width = CUTS[f]
    return (EXT, start + width) if f == 0 else (start, start + width)


EXP_STEPS = [(dy, dc) for dy in (1, 3, 2, 0) for dc in (0, 1) if (dy, dc) != (0, 0)]


def dot(a, b, dims=((1,), (0,))):
    return lax.dot_general(a, b, (dims, ((), ())), preferred_element_type=F32)


def kernel(grad_in, weights_in, ids_in, places_in, pre_in, gate_hbm, up_hbm, down_hbm, tok_out, prob_out, down_out,
           grad, weights, ids, places, pre, tok, prob, gdown,
           tokens, extras, ext_rows, frows, g, st, s, ysend, yrecv, psend, precv, xsend, xrecv, acc,
           sums, sum_ext, near_in, near_ext, single_in, single_ext, total, total_ext, far_send, far_in, far_ext,
           wgu, wdn, zsend, zrecv,
           load_sem, n_s, n_r, x_s, x_r, y_s, y_r, p_s, p_r, u_s, u_r, f_s, f_r, z_s, z_r):
    ex, et = lax.axis_index("exp"), lax.axis_index("et")
    y, core = ex // 2, ex % 2
    x, z = et // NZ, et % NZ
    odd = z % 2
    own_at = pl.multiple_of(WB + odd * WO, WO)
    other_at = pl.multiple_of(WB + (1 - odd) * WO, WO)
    column = x * 2 + z // 16
    expert = ex * 8 + column

    def at_z(dz):
        return (ex, x * NZ + lax.rem(z + dz + NZ, NZ))

    def at_x(dx):
        return (ex, lax.rem(x + dx, NX) * NZ + z)

    def exp_of(step):
        dy, dc = step
        return lax.rem(y + dy, 4) * 2 + lax.rem(core + dc, 2)

    def send(src, dst, ss, rs, device):
        copy = pltpu.make_async_remote_copy(
            src_ref=src, dst_ref=dst, send_sem=ss, recv_sem=rs, device_id=device, device_id_type=MESH)
        copy.start()
        return copy

    sent = []
    used = [0]

    def z_copy(src, dst, dz):
        i = used[0]
        used[0] += 1
        return send(src, dst, n_s.at[i], n_r.at[i], at_z(dz))

    def arrived(copies):
        for copy in copies:
            copy.wait_recv()
        sent.extend(copies)

    barrier = pltpu.get_barrier_semaphore()
    partners = [at_z(d) for d in (4, -4, 3, -3, 2, -2, 1, -1)]
    partners += [at_x(d) for d in (1, 2, 3)]
    partners += [(exp_of(step), et) for step in EXP_STEPS]
    for device in partners:
        pl.semaphore_signal(barrier, inc=1, device_id=device, device_id_type=MESH)

    early = [pltpu.make_async_copy(src, dst, load_sem.at[i]) for i, (src, dst) in enumerate(
        ((grad_in, grad), (weights_in, weights), (ids_in, ids), (places_in, places)))]
    loads = [pltpu.make_async_copy(pre_in, pre, load_sem.at[4])]
    for i, (src, dst, row) in enumerate(((gate_hbm, wgu, 0), (up_hbm, wgu, 128), (down_hbm, wdn, 0))):
        for j, (at, to, width) in enumerate(((own_at, 0, WO), (0, WO, WB), (other_at, WO + WB, WO))):
            loads.append(pltpu.make_async_copy(
                src.at[0, :, pl.ds(at, width)], dst.at[pl.ds(row, UNITS), pl.ds(to, width)],
                load_sem.at[8 + i * 3 + j]))
    for load in early + loads:
        load.start()
    for load in early:
        load.wait()
    for i in range(D // 128):
        frows[i:i + 1, :] = grad[0:1, i * 128:(i + 1) * 128].astype(F32)
    tokens[0, :, 3] = frows[0:32].reshape(2, 16, 128).astype(BF)
    extras[0, 3] = jnp.concatenate(
        [ids[...].astype(F32), places[...].astype(F32), weights[...].astype(F32),
         jnp.zeros((1, EXT - 3 * TOPK), F32)], axis=1)
    near_in[2, 1, 0] = jnp.zeros((16, 128), BF)
    pad = jnp.zeros((32, D), BF)
    wgu[pl.ds(UNITS, 32)] = pad
    wgu[pl.ds(128 + UNITS, 32)] = pad
    wdn[pl.ds(UNITS, 32)] = pad
    pl.semaphore_wait(barrier, len(partners))

    def both(cls, at, to_cls, to, count, dz):
        return [
            z_copy(tokens.at[cls, :, pl.ds(at, count)], tokens.at[to_cls, :, pl.ds(to, count)], dz),
            z_copy(extras.at[cls, pl.ds(at, count)], extras.at[to_cls, pl.ds(to, count)], dz)]

    arrived(both(0, 3, 0, 2, 1, 4) + both(0, 3, 0, 4, 1, -4))
    arrived(both(0, 3, 0, 5, 2, -8) + both(0, 2, 0, 0, 2, 8))

    arrived(
        both(0, 0, 1, 0, 7, -1) + both(0, 0, 3, 0, 7, 1)
        + [z_copy(tokens.at[0, 0, pl.ds(0, 7)], tokens.at[2, 0, pl.ds(0, 7)], -2),
           z_copy(tokens.at[0, 1, pl.ds(1, 6)], tokens.at[2, 1, pl.ds(0, 6)], 2),
           z_copy(tokens.at[0, 1, pl.ds(6, 1)], tokens.at[2, 1, pl.ds(6, 1)], -2),
           z_copy(extras.at[0, pl.ds(0, 7)], extras.at[2, pl.ds(0, 7)], -2)]
        + both(0, 0, 2, 7, 1, 2) + both(0, 0, 1, 7, 1, 3) + both(0, 6, 3, 7, 1, -3) + both(0, 6, 0, 7, 1, -4))

    for d in range(4):
        for i in range(8):
            ext_rows[d * 8 + i:d * 8 + i + 1, :] = extras[d, i]
        for h in range(2):
            frows[(d * 2 + h) * 128:(d * 2 + h + 1) * 128] = tokens[d, h].astype(F32).reshape(128, 128)
    g[0:32, 0:EXT] = ext_rows[...].astype(BF)
    gathers = []

    def unit(u):
        return jnp.concatenate(
            [frows[pl.ds((d * 2 + u // 16) * 128 + u % 16, 8, stride=16), :] for d in range(4)], axis=0)

    for f, (start, width) in enumerate(CUTS):
        begin, end = features(f)
        for col in range(begin, end, 128):
            v = (col - EXT) // 128
            if v < OWN:
                row = jnp.where(odd == 0, unit(BOTH + v), unit(BOTH + OWN + v))
            else:
                row = unit(v - OWN)
            g[0:32, col:col + 128] = row.astype(BF)
        cols = pl.ds(start, width)
        gathers.append([
            send(g.at[pl.ds(0, 32), cols], g.at[pl.ds((4 - dx) * 32, 32), cols],
                 x_s.at[dx - 1, f], x_r.at[dx - 1, f], at_x(dx))
            for dx in (1, 2, 3)])

    mine_rows = pl.ds(pl.multiple_of(ex * PAD, PAD), PAD)
    dispatch = []
    for f, (start, width) in enumerate(CUTS):
        cols = pl.ds(start, width)
        for copy in gathers[f]:
            copy.wait_recv()
        if f == 0:
            ext = g[:, 0:EXT].astype(F32)
            code = ext * 32.0 + pltpu.roll(ext, EXT - TOPK, 1)
            lane = lax.broadcasted_iota(jnp.int32, (128, ROWS), 1)
            target = ((lane // PAD) * 256 + lane % PAD + column * PAD).astype(F32)
            hit = jnp.zeros((128, ROWS), F32)
            for k in range(TOPK):
                hit = hit + jnp.where(code[:, k:k + 1] == target, 1.0, 0.0)
            st[...] = hit.astype(BF)
            s[...] = jnp.transpose(hit).astype(BF)
        ysend[:, start:start + width] = dot(s[...], g[:, start:start + width]).astype(BF)
        copies = []
        for j, step in enumerate(EXP_STEPS):
            to = exp_of(step)
            rows = pl.ds(pl.multiple_of(to * PAD, PAD), PAD)
            copies.append(send(ysend.at[rows, cols], yrecv.at[mine_rows, cols],
                               y_s.at[j, f], y_r.at[j, f], (to, et)))
        yrecv[mine_rows, start:start + width] = ysend[mine_rows, start:start + width]
        dispatch.append(copies)

    for load in loads:
        load.wait()
    slot_row = lax.broadcasted_iota(jnp.int32, (ROWS, SLOTS), 0)
    slot_col = lax.broadcasted_iota(jnp.int32, (ROWS, SLOTS), 1)
    place = (slot_row // PAD) * CAP + slot_row % PAD
    spread = jnp.where((place == slot_col) & (slot_row % PAD < CAP), 1.0, 0.0).astype(BF)
    pre_rows = dot(spread, pre[0], ((1,), (1,))).astype(BF)
    unit_row = lax.broadcasted_iota(jnp.int32, (2 * UNITS, 128), 0)
    unit_col = lax.broadcasted_iota(jnp.int32, (2 * UNITS, 128), 1)
    pick_gate = jnp.where((unit_row == unit_col) & (unit_col < UNITS), 1.0, 0.0).astype(BF)
    pick_up = jnp.where((unit_row == unit_col + UNITS) & (unit_col < UNITS), 1.0, 0.0).astype(BF)
    gate_pre = dot(pre_rows, pick_gate)
    up_pre = dot(pre_rows, pick_up)
    sig = jax.nn.sigmoid(gate_pre)
    active = gate_pre * sig
    product = active * up_pre
    hidden = product.astype(BF).astype(F32)
    gate_factor = up_pre * sig * (1.0 + gate_pre * (1.0 - sig))

    pair = at_z(1 - 2 * odd)
    half = WO // 2
    forwards = []
    back = jnp.zeros((ROWS, 128), F32)
    for f in range(NCH):
        begin, end = features(f)
        for copy in dispatch[f]:
            copy.wait_recv()
        if f < 2:
            forwards.append(send(
                yrecv.at[:, pl.ds(begin, half)], yrecv.at[:, pl.ds(WIDE + f * half, half)],
                f_s.at[f], f_r.at[f], pair))
        back = back + dot(yrecv[:, begin:end], wdn[:, begin - EXT:end - EXT], ((1,), (1,)))
        sent += dispatch[f] + gathers[f]
    for f in range(2):
        forwards[f].wait_recv()
        begin = WIDE + f * half
        back = back + dot(yrecv[:, begin:begin + half], wdn[:, begin - EXT:begin - EXT + half], ((1,), (1,)))
    sent += forwards

    ext = yrecv[:, 0:EXT].astype(F32)
    lane = lax.broadcasted_iota(jnp.int32, (ROWS, EXT), 1)
    named = (lane < TOPK) & (ext.astype(jnp.int32) == expert)
    weight = jnp.sum(jnp.where(named, pltpu.roll(ext, EXT - 2 * TOPK, 1), 0.0), axis=1, keepdims=True)
    scaled = weight * back
    grads = jnp.concatenate([scaled * gate_factor, scaled * active], axis=1).astype(BF)
    part_prob = jnp.sum(hidden * back, axis=1, keepdims=True)
    psend[:, 0:EXT] = jnp.where(named, part_prob, 0.0).astype(BF)
    weighted = jnp.transpose(weight * product).astype(BF)

    swaps = []
    for f in range(2):
        begin = WO + WB + f * half
        zsend[:, f * half:(f + 1) * half] = dot(grads, wgu[:, begin:begin + half]).astype(BF)
        part = pl.ds(f * half, half)
        swaps.append(send(zsend.at[:, part], zrecv.at[:, part], z_s.at[f], z_r.at[f], pair))
    combine = [None] * NCH
    for f in BACK_ORDER:
        start, width = CUTS[f]
        begin, end = features(f)
        cols = pl.ds(start, width)
        part = dot(grads, wgu[:, begin - EXT:end - EXT])
        if f < 2:
            swaps[f].wait_recv()
            part = part + zrecv[:, f * half:(f + 1) * half].astype(F32)
        psend[:, begin:end] = part.astype(BF)
        copies = []
        for j, step in enumerate(EXP_STEPS):
            to = exp_of(step)
            rows = pl.ds(pl.multiple_of(to * PAD, PAD), PAD)
            copies.append(send(psend.at[rows, cols], precv.at[mine_rows, cols],
                               p_s.at[j, f], p_r.at[j, f], (to, et)))
        precv[mine_rows, start:start + width] = psend[mine_rows, start:start + width]
        combine[f] = copies
        if f == 3:
            for at, begin, width in ((0, EXT + WO, WB), (own_at, EXT, WO), (other_at, WIDE, WO)):
                gdown[:, pl.ds(at, width)] = dot(weighted, yrecv[:, begin:begin + width])[0:UNITS].astype(BF)
    sent += swaps
    stores = [pltpu.make_async_copy(gdown, down_out, load_sem.at[5])]
    stores[0].start()

    reduces = [None] * NCH
    for f in BACK_ORDER:
        start, width = CUTS[f]
        cols = pl.ds(start, width)
        for copy in combine[f]:
            copy.wait_recv()
        sent += combine[f]
        dense = dot(st[...], precv[:, start:start + width])
        acc[:, start:start + width] = dense[0:32]
        xsend[:, start:start + width] = dense[32:128].astype(BF)
        reduces[f] = [
            send(xsend.at[pl.ds((dx - 1) * 32, 32), cols], xrecv.at[dx - 1, :, cols],
                 u_s.at[dx - 1, f], u_r.at[dx - 1, f], at_x(dx))
            for dx in (1, 2, 3)]

    def put(u, rows):
        for d in range(4):
            frows[pl.ds((d * 2 + u // 16) * 128 + u % 16, 8, stride=16), :] = rows[d * 8:d * 8 + 8]

    for f in BACK_ORDER:
        start, width = CUTS[f]
        begin, end = features(f)
        for copy in reduces[f]:
            copy.wait_recv()
        sent += reduces[f]
        whole = acc[:, start:start + width]
        for i in range(3):
            whole = whole + xrecv[i, :, start:start + width].astype(F32)
        if f == 0:
            ext_total = whole[:, 0:EXT]
        for col in range(begin, end, 128):
            v = (col - EXT) // 128
            rows = whole[:, col - start:col - start + 128]
            if v < OWN:
                put(BOTH + v, jnp.where(odd == 0, rows, 0.0))
                put(BOTH + OWN + v, jnp.where(odd == 0, 0.0, rows))
            else:
                put(v - OWN, rows)

    for d in range(4):
        for h in range(2):
            if d:
                sums[d, h] = frows[(d * 2 + h) * 128:(d * 2 + h + 1) * 128].reshape(8, 16, 128).astype(BF)
            else:
                sums[d, h, 7] = frows[h * 128 + 112:h * 128 + 128].astype(BF)
        for i in range(8):
            sum_ext[d, i] = ext_total[d * 8 + i:d * 8 + i + 1]

    def seven(cls, to, dz):
        return [z_copy(sums.at[cls, :, pl.ds(0, 7)], near_in.at[to, :, pl.ds(0, 7)], dz),
                z_copy(sum_ext.at[cls, pl.ds(0, 7)], near_ext.at[to], dz)]

    def eighth(cls, to, dz):
        return [z_copy(sums.at[cls, :, pl.ds(7, 1)], single_in.at[to], dz),
                z_copy(sum_ext.at[cls, pl.ds(7, 1)], single_ext.at[to], dz)]

    arrived(
        seven(1, 0, 1) + seven(3, 1, -1)
        + [z_copy(sums.at[2, 0, pl.ds(0, 7)], near_in.at[2, 0, pl.ds(0, 7)], 2),
           z_copy(sums.at[2, 1, pl.ds(0, 6)], near_in.at[2, 1, pl.ds(1, 6)], -2),
           z_copy(sums.at[2, 1, pl.ds(6, 1)], single_in.at[4, 1], 2),
           z_copy(sum_ext.at[2, pl.ds(0, 7)], near_ext.at[2], 2)]
        + eighth(2, 0, -2) + eighth(1, 1, -3) + eighth(3, 2, 3) + eighth(0, 3, 4))
    for h in range(2):
        rows = frows[h * 128:h * 128 + 112].reshape(7, 16, 128)
        for i in range(3):
            rows = rows + near_in[i, h, 0:7].astype(F32)
        total[h] = rows
    rows = sum_ext[0, 0:7]
    for i in range(3):
        rows = rows + near_ext[i]
    total_ext[...] = rows
    for place, left in ((0, (0, 1)), (6, (2, 3))):
        for i in left:
            total[:, place] = total[:, place] + single_in[i, :, 0].astype(F32)
            total_ext[place] = total_ext[place] + single_ext[i, 0]
    total[1, 6] = total[1, 6] + single_in[4, 1, 0].astype(F32)

    far_send[...] = total[...].astype(BF)

    def back_far(at, to, count, dz):
        return [z_copy(far_send.at[:, pl.ds(at, count)], far_in.at[to, :, pl.ds(0, count)], dz),
                z_copy(total_ext.at[pl.ds(at, count)], far_ext.at[to, pl.ds(0, count)], dz)]

    arrived(back_far(5, 0, 2, 8) + back_far(0, 1, 2, -8))
    far_send[:, 2] = (total[:, 2] + far_in[1, :, 0].astype(F32)).astype(BF)
    far_send[:, 4] = (total[:, 4] + far_in[0, :, 1].astype(F32)).astype(BF)
    last = total[:, 3] + far_in[0, :, 0].astype(F32) + far_in[1, :, 1].astype(F32)
    last_ext = total_ext[3] + far_ext[0, 0] + far_ext[1, 1]
    far_ext[2, 1] = total_ext[2] + far_ext[1, 0]
    far_ext[3, 1] = total_ext[4] + far_ext[0, 1]
    arrived([
        z_copy(far_send.at[:, pl.ds(2, 1)], far_in.at[2, :, pl.ds(0, 1)], -4),
        z_copy(far_ext.at[2, pl.ds(1, 1)], far_ext.at[2, pl.ds(0, 1)], -4),
        z_copy(far_send.at[:, pl.ds(4, 1)], far_in.at[3, :, pl.ds(0, 1)], 4),
        z_copy(far_ext.at[3, pl.ds(1, 1)], far_ext.at[3, pl.ds(0, 1)], 4)])
    last = last + far_in[2, :, 0].astype(F32) + far_in[3, :, 0].astype(F32)
    last_ext = last_ext + far_ext[2, 0] + far_ext[3, 0]
    frows[0:32] = last.reshape(32, 128)
    for i in range(D // 128):
        tok[0:1, i * 128:(i + 1) * 128] = frows[i:i + 1, :].astype(BF)
    prob[...] = last_ext[:, 0:TOPK]
    for i, (src, dst) in enumerate(((tok, tok_out), (prob, prob_out))):
        stores.append(pltpu.make_async_copy(src, dst, load_sem.at[6 + i]))
        stores[-1].start()
    for copy in sent:
        copy.wait_send()
    for store in stores:
        store.wait()


def deliver(tok, prob, down, tok_out, prob_out, down_out, tok_buf, prob_buf, down_buf, in_sem, out_sem):
    parts = [(tok, tok_buf, tok_out), (prob, prob_buf, prob_out)]
    for i in range(0, UNITS, 32):
        rows = pl.ds(i, 32)
        parts.append((down.at[rows], down_buf.at[rows], down_out.at[rows]))
    ins = [pltpu.make_async_copy(src, buf, in_sem.at[i]) for i, (src, buf, _) in enumerate(parts)]
    outs = [pltpu.make_async_copy(buf, dst, out_sem.at[i]) for i, (_, buf, dst) in enumerate(parts)]
    for copy in ins:
        copy.start()
    for copy, onward in zip(ins, outs):
        copy.wait()
        onward.start()
    for copy in outs:
        copy.wait()


def body(grad_out, route_weight, expert_ids, slot_ids, saved_pre, gate_proj, up_proj, down_proj):
    hbm = pl.BlockSpec(memory_space=pl.ANY)
    dma = lambda *shape: pltpu.SemaphoreType.DMA(shape)
    outs = (
        jax.ShapeDtypeStruct((1, D), BF),
        jax.ShapeDtypeStruct((1, TOPK), F32),
        jax.ShapeDtypeStruct((UNITS, D), BF),
    )
    results = pl.pallas_call(
        kernel,
        out_shape=outs,
        in_specs=[hbm] * 8,
        out_specs=(hbm,) * 3,
        scratch_shapes=[
            pltpu.VMEM((1, D), BF),
            pltpu.VMEM((1, TOPK), BF),
            pltpu.VMEM((1, TOPK), jnp.int32),
            pltpu.VMEM((1, TOPK), jnp.int32),
            pltpu.VMEM((1, 2 * UNITS, SLOTS), BF),
            pltpu.VMEM((1, D), BF),
            pltpu.VMEM((1, TOPK), F32),
            pltpu.VMEM((UNITS, D), BF),
            pltpu.VMEM((4, 2, 8, 16, 128), BF),
            pltpu.VMEM((4, 8, 1, 128), F32),
            pltpu.VMEM((32, 128), F32),
            pltpu.VMEM((1024, 128), F32),
            pltpu.VMEM((128, WIDE), BF),
            pltpu.VMEM((128, ROWS), BF),
            pltpu.VMEM((ROWS, 128), BF),
            pltpu.VMEM((ROWS, WIDE), BF),
            pltpu.VMEM((ROWS, EXT + D), BF),
            pltpu.VMEM((ROWS, WIDE), BF),
            pltpu.VMEM((ROWS, WIDE), BF),
            pltpu.VMEM((96, WIDE), BF),
            pltpu.VMEM((3, 32, WIDE), BF),
            pltpu.VMEM((32, WIDE), F32),
            pltpu.VMEM((4, 2, 8, 16, 128), BF),
            pltpu.VMEM((4, 8, 1, 128), F32),
            pltpu.VMEM((3, 2, 7, 16, 128), BF),
            pltpu.VMEM((3, 7, 1, 128), F32),
            pltpu.VMEM((5, 2, 1, 16, 128), BF),
            pltpu.VMEM((4, 1, 1, 128), F32),
            pltpu.VMEM((2, 7, 16, 128), F32),
            pltpu.VMEM((7, 1, 128), F32),
            pltpu.VMEM((2, 7, 16, 128), BF),
            pltpu.VMEM((4, 2, 2, 16, 128), BF),
            pltpu.VMEM((4, 2, 1, 128), F32),
            pltpu.VMEM((256, D), BF),
            pltpu.VMEM((128, D), BF),
            pltpu.VMEM((ROWS, WO), BF),
            pltpu.VMEM((ROWS, WO), BF),
            dma(17), dma(64), dma(64), dma(3, NCH), dma(3, NCH), dma(7, NCH), dma(7, NCH),
            dma(7, NCH), dma(7, NCH), dma(3, NCH), dma(3, NCH),
            dma(2), dma(2), dma(2), dma(2),
        ],
        compiler_params=pltpu.CompilerParams(
            collective_id=0, has_side_effects=True, vmem_limit_bytes=60 * 2**20),
    )(grad_out, route_weight, expert_ids, slot_ids, jnp.swapaxes(saved_pre, 1, 2), gate_proj, up_proj, down_proj)
    tokens, probs, down_grad = pl.pallas_call(
        deliver,
        out_shape=outs,
        in_specs=[hbm] * 3,
        out_specs=(hbm,) * 3,
        scratch_shapes=[
            pltpu.VMEM((1, D), BF), pltpu.VMEM((1, TOPK), F32), pltpu.VMEM((UNITS, D), BF), dma(5), dma(5)],
    )(*results)
    return tokens, probs, down_grad[None]


def solution(mesh):
    rows, blocks = P(("exp", "et"), None), P(("exp", "et"), None, None)
    return jax.shard_map(
        body, mesh=mesh, in_specs=(rows, rows, rows, rows, blocks, blocks, blocks, blocks),
        out_specs=(rows, rows, blocks), check_vma=False)
```

```python
import jax
import jax.numpy as jnp
from jax import lax
from jax.experimental import pallas as pl
from jax.experimental.pallas import tpu as pltpu
from jax.sharding import PartitionSpec as P

MESH = pl.DeviceIdType.MESH
BF, F32 = jnp.bfloat16, jnp.float32
D, UNITS, TOPK, CAP = 4096, 96, 8, 30
SLOTS, PAD, BLOCKS = 240, 32, 8
ROWS = BLOCKS * PAD
EXT = 128
NX, NZ = 4, 32
OWN, BOTH = 8, 16
WO, WB = OWN * 128, BOTH * 128
WIDE = EXT + WO + WB
CUTS = [(0, EXT + WO // 2), (EXT + WO // 2, WO // 2), (EXT + WO, WB // 2), (EXT + WO + WB // 2, WB // 2)]
NCH = len(CUTS)
BACK_ORDER = (2, 3, 0, 1)


def features(f):
    start, width = CUTS[f]
    return (EXT, start + width) if f == 0 else (start, start + width)


EXP_STEPS = [(dy, dc) for dy in (1, 3, 2, 0) for dc in (0, 1) if (dy, dc) != (0, 0)]


def dot(a, b, dims=((1,), (0,))):
    return lax.dot_general(a, b, (dims, ((), ())), preferred_element_type=F32)


def kernel(grad_in, weights_in, ids_in, places_in, pre_in, gate_hbm, up_hbm, down_hbm, tok_out, prob_out, down_out,
           grad, weights, ids, places, pre, tok, prob, gdown,
           tokens, extras, ext_rows, frows, g, st, s, ysend, yrecv, psend, precv, xsend, xrecv, acc,
           sums, sum_ext, near_in, near_ext, single_in, single_ext, total, total_ext, far_send, far_in, far_ext,
           wgu, wdn, zsend, zrecv,
           load_sem, n_s, n_r, x_s, x_r, y_s, y_r, p_s, p_r, u_s, u_r, f_s, f_r, z_s, z_r):
    ex, et = lax.axis_index("exp"), lax.axis_index("et")
    y, core = ex // 2, ex % 2
    x, z = et // NZ, et % NZ
    odd = z % 2
    own_at = pl.multiple_of(WB + odd * WO, WO)
    other_at = pl.multiple_of(WB + (1 - odd) * WO, WO)
    column = x * 2 + z // 16
    expert = ex * 8 + column

    def at_z(dz):
        return (ex, x * NZ + lax.rem(z + dz + NZ, NZ))

    def at_x(dx):
        return (ex, lax.rem(x + dx, NX) * NZ + z)

    def exp_of(step):
        dy, dc = step
        return lax.rem(y + dy, 4) * 2 + lax.rem(core + dc, 2)

    def send(src, dst, ss, rs, device):
        copy = pltpu.make_async_remote_copy(
            src_ref=src, dst_ref=dst, send_sem=ss, recv_sem=rs, device_id=device, device_id_type=MESH)
        copy.start()
        return copy

    sent = []
    used = [0]

    def z_copy(src, dst, dz):
        i = used[0]
        used[0] += 1
        return send(src, dst, n_s.at[i], n_r.at[i], at_z(dz))

    def arrived(copies):
        for copy in copies:
            copy.wait_recv()
        sent.extend(copies)

    barrier = pltpu.get_barrier_semaphore()
    partners = [at_z(d) for d in (4, -4, 3, -3, 2, -2, 1, -1)]
    partners += [at_x(d) for d in (1, 2, 3)]
    partners += [(exp_of(step), et) for step in EXP_STEPS]
    for device in partners:
        pl.semaphore_signal(barrier, inc=1, device_id=device, device_id_type=MESH)

    early = [pltpu.make_async_copy(src, dst, load_sem.at[i]) for i, (src, dst) in enumerate(
        ((grad_in, grad), (weights_in, weights), (ids_in, ids), (places_in, places)))]
    loads = [pltpu.make_async_copy(pre_in, pre, load_sem.at[4])]
    for i, (src, dst, row) in enumerate(((gate_hbm, wgu, 0), (up_hbm, wgu, 128), (down_hbm, wdn, 0))):
        for j, (at, to, width) in enumerate(((own_at, 0, WO), (0, WO, WB), (other_at, WO + WB, WO))):
            loads.append(pltpu.make_async_copy(
                src.at[0, :, pl.ds(at, width)], dst.at[pl.ds(row, UNITS), pl.ds(to, width)],
                load_sem.at[8 + i * 3 + j]))
    for load in early + loads:
        load.start()
    for load in early:
        load.wait()
    for i in range(D // 128):
        frows[i:i + 1, :] = grad[0:1, i * 128:(i + 1) * 128].astype(F32)
    tokens[0, :, 3] = frows[0:32].reshape(2, 16, 128).astype(BF)
    extras[0, 3] = jnp.concatenate(
        [ids[...].astype(F32), places[...].astype(F32), weights[...].astype(F32),
         jnp.zeros((1, EXT - 3 * TOPK), F32)], axis=1)
    near_in[2, 1, 0] = jnp.zeros((16, 128), BF)
    pad = jnp.zeros((32, D), BF)
    wgu[pl.ds(UNITS, 32)] = pad
    wgu[pl.ds(128 + UNITS, 32)] = pad
    wdn[pl.ds(UNITS, 32)] = pad
    pl.semaphore_wait(barrier, len(partners))

    def feats(h, cls, at, to_cls, to, count, dz):
        return z_copy(tokens.at[cls, h, pl.ds(at, count)], tokens.at[to_cls, h, pl.ds(to, count)], dz)

    def sides(cls, at, to_cls, to, count, dz):
        return z_copy(extras.at[cls, pl.ds(at, count)], extras.at[to_cls, pl.ds(to, count)], dz)

    def move(h, moves):
        return [feats(h, *m) for m in moves] + ([sides(*m) for m in moves] if h else [])

    halves = (1, 0)
    quarter = {h: move(h, [(0, 3, 0, 2, 1, 4), (0, 3, 0, 4, 1, -4)]) for h in halves}
    eighths, near = {}, {}
    for h in halves:
        arrived(quarter[h])
        eighths[h] = move(h, [(0, 3, 0, 5, 2, -8), (0, 2, 0, 0, 2, 8)])

    for h in halves:
        arrived(eighths[h])
        near[h] = move(h, [(0, 6, 0, 7, 1, -4), (0, 0, 1, 7, 1, 3), (0, 6, 3, 7, 1, -3), (0, 0, 2, 7, 1, 2),
                           (0, 0, 1, 0, 7, -1), (0, 0, 3, 0, 7, 1)])
        if h:
            near[h] += [feats(h, 0, 1, 2, 0, 6, 2), feats(h, 0, 6, 2, 6, 1, -2), sides(0, 0, 2, 0, 7, -2)]
        else:
            near[h] += [feats(h, 0, 0, 2, 0, 7, -2)]

    def spread_rows(h):
        arrived(near[h])
        for d in range(4):
            frows[(d * 2 + h) * 128:(d * 2 + h + 1) * 128] = tokens[d, h].astype(F32).reshape(128, 128)

    spread_rows(1)
    for d in range(4):
        for i in range(8):
            ext_rows[d * 8 + i:d * 8 + i + 1, :] = extras[d, i]
    g[0:32, 0:EXT] = ext_rows[...].astype(BF)
    gathers = []

    def unit(u):
        return jnp.concatenate(
            [frows[pl.ds((d * 2 + u // 16) * 128 + u % 16, 8, stride=16), :] for d in range(4)], axis=0)

    for f, (start, width) in enumerate(CUTS):
        begin, end = features(f)
        if f == 2:
            spread_rows(0)
        for col in range(begin, end, 128):
            v = (col - EXT) // 128
            if v < OWN:
                row = jnp.where(odd == 0, unit(BOTH + v), unit(BOTH + OWN + v))
            else:
                row = unit(v - OWN)
            g[0:32, col:col + 128] = row.astype(BF)
        cols = pl.ds(start, width)
        gathers.append([
            send(g.at[pl.ds(0, 32), cols], g.at[pl.ds((4 - dx) * 32, 32), cols],
                 x_s.at[dx - 1, f], x_r.at[dx - 1, f], at_x(dx))
            for dx in (1, 2, 3)])

    mine_rows = pl.ds(pl.multiple_of(ex * PAD, PAD), PAD)
    dispatch = []
    for f, (start, width) in enumerate(CUTS):
        cols = pl.ds(start, width)
        for copy in gathers[f]:
            copy.wait_recv()
        if f == 0:
            ext = g[:, 0:EXT].astype(F32)
            code = ext * 32.0 + pltpu.roll(ext, EXT - TOPK, 1)
            lane = lax.broadcasted_iota(jnp.int32, (128, ROWS), 1)
            target = ((lane // PAD) * 256 + lane % PAD + column * PAD).astype(F32)
            hit = jnp.zeros((128, ROWS), F32)
            for k in range(TOPK):
                hit = hit + jnp.where(code[:, k:k + 1] == target, 1.0, 0.0)
            st[...] = hit.astype(BF)
            s[...] = jnp.transpose(hit).astype(BF)
        ysend[:, start:start + width] = dot(s[...], g[:, start:start + width]).astype(BF)
        copies = []
        for j, step in enumerate(EXP_STEPS):
            to = exp_of(step)
            rows = pl.ds(pl.multiple_of(to * PAD, PAD), PAD)
            copies.append(send(ysend.at[rows, cols], yrecv.at[mine_rows, cols],
                               y_s.at[j, f], y_r.at[j, f], (to, et)))
        yrecv[mine_rows, start:start + width] = ysend[mine_rows, start:start + width]
        dispatch.append(copies)

    for load in loads:
        load.wait()
    slot_row = lax.broadcasted_iota(jnp.int32, (ROWS, SLOTS), 0)
    slot_col = lax.broadcasted_iota(jnp.int32, (ROWS, SLOTS), 1)
    place = (slot_row // PAD) * CAP + slot_row % PAD
    spread = jnp.where((place == slot_col) & (slot_row % PAD < CAP), 1.0, 0.0).astype(BF)
    pre_rows = dot(spread, pre[0], ((1,), (1,))).astype(BF)
    unit_row = lax.broadcasted_iota(jnp.int32, (2 * UNITS, 128), 0)
    unit_col = lax.broadcasted_iota(jnp.int32, (2 * UNITS, 128), 1)
    pick_gate = jnp.where((unit_row == unit_col) & (unit_col < UNITS), 1.0, 0.0).astype(BF)
    pick_up = jnp.where((unit_row == unit_col + UNITS) & (unit_col < UNITS), 1.0, 0.0).astype(BF)
    gate_pre = dot(pre_rows, pick_gate)
    up_pre = dot(pre_rows, pick_up)
    sig = jax.nn.sigmoid(gate_pre)
    active = gate_pre * sig
    product = active * up_pre
    hidden = product.astype(BF).astype(F32)
    gate_factor = up_pre * sig * (1.0 + gate_pre * (1.0 - sig))

    pair = at_z(1 - 2 * odd)
    half = WO // 2
    forwards = []
    back = jnp.zeros((ROWS, 128), F32)
    for f in range(NCH):
        begin, end = features(f)
        for copy in dispatch[f]:
            copy.wait_recv()
        if f < 2:
            forwards.append(send(
                yrecv.at[:, pl.ds(begin, half)], yrecv.at[:, pl.ds(WIDE + f * half, half)],
                f_s.at[f], f_r.at[f], pair))
        back = back + dot(yrecv[:, begin:end], wdn[:, begin - EXT:end - EXT], ((1,), (1,)))
        sent += dispatch[f] + gathers[f]
    for f in range(2):
        forwards[f].wait_recv()
        begin = WIDE + f * half
        back = back + dot(yrecv[:, begin:begin + half], wdn[:, begin - EXT:begin - EXT + half], ((1,), (1,)))
    sent += forwards

    ext = yrecv[:, 0:EXT].astype(F32)
    lane = lax.broadcasted_iota(jnp.int32, (ROWS, EXT), 1)
    named = (lane < TOPK) & (ext.astype(jnp.int32) == expert)
    weight = jnp.sum(jnp.where(named, pltpu.roll(ext, EXT - 2 * TOPK, 1), 0.0), axis=1, keepdims=True)
    scaled = weight * back
    grads = jnp.concatenate([scaled * gate_factor, scaled * active], axis=1).astype(BF)
    part_prob = jnp.sum(hidden * back, axis=1, keepdims=True)
    psend[:, 0:EXT] = jnp.where(named, part_prob, 0.0).astype(BF)
    weighted = jnp.transpose(weight * product).astype(BF)

    swaps = []
    for f in range(2):
        begin = WO + WB + f * half
        zsend[:, f * half:(f + 1) * half] = dot(grads, wgu[:, begin:begin + half]).astype(BF)
        part = pl.ds(f * half, half)
        swaps.append(send(zsend.at[:, part], zrecv.at[:, part], z_s.at[f], z_r.at[f], pair))
    combine = [None] * NCH
    for f in BACK_ORDER:
        start, width = CUTS[f]
        begin, end = features(f)
        cols = pl.ds(start, width)
        part = dot(grads, wgu[:, begin - EXT:end - EXT])
        if f < 2:
            swaps[f].wait_recv()
            part = part + zrecv[:, f * half:(f + 1) * half].astype(F32)
        psend[:, begin:end] = part.astype(BF)
        copies = []
        for j, step in enumerate(EXP_STEPS):
            to = exp_of(step)
            rows = pl.ds(pl.multiple_of(to * PAD, PAD), PAD)
            copies.append(send(psend.at[rows, cols], precv.at[mine_rows, cols],
                               p_s.at[j, f], p_r.at[j, f], (to, et)))
        precv[mine_rows, start:start + width] = psend[mine_rows, start:start + width]
        combine[f] = copies
        if f == 3:
            for at, begin, width in ((0, EXT + WO, WB), (own_at, EXT, WO), (other_at, WIDE, WO)):
                gdown[:, pl.ds(at, width)] = dot(weighted, yrecv[:, begin:begin + width])[0:UNITS].astype(BF)
    sent += swaps
    stores = [pltpu.make_async_copy(gdown, down_out, load_sem.at[5])]
    stores[0].start()

    reduces = [None] * NCH

    def combine_rows(f):
        start, width = CUTS[f]
        cols = pl.ds(start, width)
        arrived(combine[f])
        dense = dot(st[...], precv[:, start:start + width])
        acc[:, start:start + width] = dense[0:32]
        xsend[:, start:start + width] = dense[32:128].astype(BF)
        reduces[f] = [
            send(xsend.at[pl.ds((dx - 1) * 32, 32), cols], xrecv.at[dx - 1, :, cols],
                 u_s.at[dx - 1, f], u_r.at[dx - 1, f], at_x(dx))
            for dx in (1, 2, 3)]

    def put(u, rows):
        for d in range(4):
            frows[pl.ds((d * 2 + u // 16) * 128 + u % 16, 8, stride=16), :] = rows[d * 8:d * 8 + 8]

    def sum_rows(f):
        start, width = CUTS[f]
        begin, end = features(f)
        arrived(reduces[f])
        whole = acc[:, start:start + width]
        for i in range(3):
            whole = whole + xrecv[i, :, start:start + width].astype(F32)
        if f == 0:
            for d in range(4):
                for i in range(8):
                    sum_ext[d, i] = whole[d * 8 + i:d * 8 + i + 1, 0:EXT]
        for col in range(begin, end, 128):
            v = (col - EXT) // 128
            rows = whole[:, col - start:col - start + 128]
            if v < OWN:
                put(BOTH + v, jnp.where(odd == 0, rows, 0.0))
                put(BOTH + OWN + v, jnp.where(odd == 0, 0.0, rows))
            else:
                put(v - OWN, rows)

    def send_near(h):
        for d in range(4):
            if d:
                sums[d, h] = frows[(d * 2 + h) * 128:(d * 2 + h + 1) * 128].reshape(8, 16, 128).astype(BF)
            else:
                sums[d, h, 7] = frows[h * 128 + 112:h * 128 + 128].astype(BF)
        copies = []
        for cls, to, dz in ((0, 3, 4), (1, 1, -3), (3, 2, 3), (2, 0, -2)):
            copies.append(z_copy(sums.at[cls, h, pl.ds(7, 1)], single_in.at[to, h], dz))
            if h:
                copies.append(z_copy(sum_ext.at[cls, pl.ds(7, 1)], single_ext.at[to], dz))
        for cls, to, dz in ((1, 0, 1), (3, 1, -1), (2, 2, 2)):
            if cls != 2 or h == 0:
                copies.append(z_copy(sums.at[cls, h, pl.ds(0, 7)], near_in.at[to, h, pl.ds(0, 7)], dz))
            if h:
                copies.append(z_copy(sum_ext.at[cls, pl.ds(0, 7)], near_ext.at[to], dz))
        if h:
            copies.append(z_copy(sums.at[2, 1, pl.ds(0, 6)], near_in.at[2, 1, pl.ds(1, 6)], -2))
            copies.append(z_copy(sums.at[2, 1, pl.ds(6, 1)], single_in.at[4, 1], 2))
        return copies

    combine_rows(2)
    combine_rows(3)
    combine_rows(0)
    sum_rows(2)
    sum_rows(3)
    near = {0: send_near(0)}
    combine_rows(1)
    sum_rows(0)
    sum_rows(1)
    near[1] = send_near(1)

    def send_far(h):
        arrived(near[h])
        rows = frows[h * 128:h * 128 + 112].reshape(7, 16, 128)
        for i in range(3):
            rows = rows + near_in[i, h, 0:7].astype(F32)
        total[h] = rows
        for place, left in ((0, (0, 1)), (6, (2, 3))):
            for i in left:
                total[h, place] = total[h, place] + single_in[i, h, 0].astype(F32)
        if h:
            total[1, 6] = total[1, 6] + single_in[4, 1, 0].astype(F32)
            rows = sum_ext[0, 0:7]
            for i in range(3):
                rows = rows + near_ext[i]
            total_ext[...] = rows
            for place, left in ((0, (0, 1)), (6, (2, 3))):
                for i in left:
                    total_ext[place] = total_ext[place] + single_ext[i, 0]
        far_send[h] = total[h].astype(BF)
        copies = []
        for at, to, dz in ((5, 0, 8), (0, 1, -8)):
            copies.append(z_copy(far_send.at[h, pl.ds(at, 2)], far_in.at[to, h], dz))
            if h:
                copies.append(z_copy(total_ext.at[pl.ds(at, 2)], far_ext.at[to], dz))
        return copies

    far = {h: send_far(h) for h in (0, 1)}

    def send_last(h):
        arrived(far[h])
        far_send[h, 2] = (total[h, 2] + far_in[1, h, 0].astype(F32)).astype(BF)
        far_send[h, 4] = (total[h, 4] + far_in[0, h, 1].astype(F32)).astype(BF)
        total[h, 3] = total[h, 3] + far_in[0, h, 0].astype(F32) + far_in[1, h, 1].astype(F32)
        if h:
            total_ext[2] = total_ext[2] + far_ext[1, 0]
            total_ext[4] = total_ext[4] + far_ext[0, 1]
            total_ext[3] = total_ext[3] + far_ext[0, 0] + far_ext[1, 1]
        copies = []
        for at, to, dz in ((2, 2, -4), (4, 3, 4)):
            copies.append(z_copy(far_send.at[h, pl.ds(at, 1)], far_in.at[to, h, pl.ds(0, 1)], dz))
            if h:
                copies.append(z_copy(total_ext.at[pl.ds(at, 1)], far_ext.at[to, pl.ds(0, 1)], dz))
        return copies

    last = {h: send_last(h) for h in (0, 1)}
    for h in (0, 1):
        arrived(last[h])
        frows[h * 16:h * 16 + 16] = total[h, 3] + far_in[2, h, 0].astype(F32) + far_in[3, h, 0].astype(F32)
    for i in range(D // 128):
        tok[0:1, i * 128:(i + 1) * 128] = frows[i:i + 1, :].astype(BF)
    prob[...] = (total_ext[3] + far_ext[2, 0] + far_ext[3, 0])[:, 0:TOPK]
    for i, (src, dst) in enumerate(((tok, tok_out), (prob, prob_out))):
        stores.append(pltpu.make_async_copy(src, dst, load_sem.at[6 + i]))
        stores[-1].start()
    for copy in sent:
        copy.wait_send()
    for store in stores:
        store.wait()


def deliver(tok, prob, down, tok_out, prob_out, down_out, tok_buf, prob_buf, down_buf, in_sem, out_sem):
    parts = [(tok, tok_buf, tok_out), (prob, prob_buf, prob_out)]
    for i in range(0, UNITS, 32):
        rows = pl.ds(i, 32)
        parts.append((down.at[rows], down_buf.at[rows], down_out.at[rows]))
    ins = [pltpu.make_async_copy(src, buf, in_sem.at[i]) for i, (src, buf, _) in enumerate(parts)]
    outs = [pltpu.make_async_copy(buf, dst, out_sem.at[i]) for i, (_, buf, dst) in enumerate(parts)]
    for copy in ins:
        copy.start()
    for copy, onward in zip(ins, outs):
        copy.wait()
        onward.start()
    for copy in outs:
        copy.wait()


def body(grad_out, route_weight, expert_ids, slot_ids, saved_pre, gate_proj, up_proj, down_proj):
    hbm = pl.BlockSpec(memory_space=pl.ANY)
    dma = lambda *shape: pltpu.SemaphoreType.DMA(shape)
    outs = (
        jax.ShapeDtypeStruct((1, D), BF),
        jax.ShapeDtypeStruct((1, TOPK), F32),
        jax.ShapeDtypeStruct((UNITS, D), BF),
    )
    results = pl.pallas_call(
        kernel,
        out_shape=outs,
        in_specs=[hbm] * 8,
        out_specs=(hbm,) * 3,
        scratch_shapes=[
            pltpu.VMEM((1, D), BF),
            pltpu.VMEM((1, TOPK), BF),
            pltpu.VMEM((1, TOPK), jnp.int32),
            pltpu.VMEM((1, TOPK), jnp.int32),
            pltpu.VMEM((1, 2 * UNITS, SLOTS), BF),
            pltpu.VMEM((1, D), BF),
            pltpu.VMEM((1, TOPK), F32),
            pltpu.VMEM((UNITS, D), BF),
            pltpu.VMEM((4, 2, 8, 16, 128), BF),
            pltpu.VMEM((4, 8, 1, 128), F32),
            pltpu.VMEM((32, 128), F32),
            pltpu.VMEM((1024, 128), F32),
            pltpu.VMEM((128, WIDE), BF),
            pltpu.VMEM((128, ROWS), BF),
            pltpu.VMEM((ROWS, 128), BF),
            pltpu.VMEM((ROWS, WIDE), BF),
            pltpu.VMEM((ROWS, EXT + D), BF),
            pltpu.VMEM((ROWS, WIDE), BF),
            pltpu.VMEM((ROWS, WIDE), BF),
            pltpu.VMEM((96, WIDE), BF),
            pltpu.VMEM((3, 32, WIDE), BF),
            pltpu.VMEM((32, WIDE), F32),
            pltpu.VMEM((4, 2, 8, 16, 128), BF),
            pltpu.VMEM((4, 8, 1, 128), F32),
            pltpu.VMEM((3, 2, 7, 16, 128), BF),
            pltpu.VMEM((3, 7, 1, 128), F32),
            pltpu.VMEM((5, 2, 1, 16, 128), BF),
            pltpu.VMEM((4, 1, 1, 128), F32),
            pltpu.VMEM((2, 7, 16, 128), F32),
            pltpu.VMEM((7, 1, 128), F32),
            pltpu.VMEM((2, 7, 16, 128), BF),
            pltpu.VMEM((4, 2, 2, 16, 128), BF),
            pltpu.VMEM((4, 2, 1, 128), F32),
            pltpu.VMEM((256, D), BF),
            pltpu.VMEM((128, D), BF),
            pltpu.VMEM((ROWS, WO), BF),
            pltpu.VMEM((ROWS, WO), BF),
            dma(17), dma(96), dma(96), dma(3, NCH), dma(3, NCH), dma(7, NCH), dma(7, NCH),
            dma(7, NCH), dma(7, NCH), dma(3, NCH), dma(3, NCH),
            dma(2), dma(2), dma(2), dma(2),
        ],
        compiler_params=pltpu.CompilerParams(
            collective_id=0, has_side_effects=True, vmem_limit_bytes=60 * 2**20),
    )(grad_out, route_weight, expert_ids, slot_ids, jnp.swapaxes(saved_pre, 1, 2), gate_proj, up_proj, down_proj)
    tokens, probs, down_grad = pl.pallas_call(
        deliver,
        out_shape=outs,
        in_specs=[hbm] * 3,
        out_specs=(hbm,) * 3,
        scratch_shapes=[
            pltpu.VMEM((1, D), BF), pltpu.VMEM((1, TOPK), F32), pltpu.VMEM((UNITS, D), BF), dma(5), dma(5)],
    )(*results)
    return tokens, probs, down_grad[None]


def solution(mesh):
    rows, blocks = P(("exp", "et"), None), P(("exp", "et"), None, None)
    return jax.shard_map(
        body, mesh=mesh, in_specs=(rows, rows, rows, rows, blocks, blocks, blocks, blocks),
        out_specs=(rows, rows, blocks), check_vma=False)
```

```python
import jax
import jax.numpy as jnp
from jax import lax
from jax.experimental import pallas as pl
from jax.experimental.pallas import tpu as pltpu
from jax.sharding import PartitionSpec as P

MESH = pl.DeviceIdType.MESH
BF, F32 = jnp.bfloat16, jnp.float32
D, UNITS, TOPK, CAP = 4096, 96, 8, 30
SLOTS, PAD, BLOCKS = 240, 32, 8
ROWS = BLOCKS * PAD
EXT = 128
NX, NZ = 4, 32
OWN, BOTH = 8, 16
WO, WB = OWN * 128, BOTH * 128
WIDE = EXT + WO + WB
FIRST = 2 * 128
PARTS = [(0, FIRST), (FIRST, WO - FIRST)]
CUTS = [(0, EXT + FIRST), (EXT + FIRST, WO - FIRST), (EXT + WO, WB // 2), (EXT + WO + WB // 2, WB // 2)]
NCH = len(CUTS)
BACK_ORDER = (2, 3, 1, 0)


def features(f):
    start, width = CUTS[f]
    return (EXT, start + width) if f == 0 else (start, start + width)


EXP_STEPS = [(dy, dc) for dy in (1, 3, 2, 0) for dc in (0, 1) if (dy, dc) != (0, 0)]


def dot(a, b, dims=((1,), (0,))):
    return lax.dot_general(a, b, (dims, ((), ())), preferred_element_type=F32)


def kernel(grad_in, weights_in, ids_in, places_in, pre_in, gate_hbm, up_hbm, down_hbm, tok_out, prob_out, down_out,
           grad, weights, ids, places, pre, tok, prob, gdown,
           tokens, extras, ext_rows, frows, g, st, s, ysend, yrecv, psend, precv, xsend, xrecv, acc,
           sums, sum_ext, near_in, near_ext, single_in, single_ext, total, total_ext, far_send, far_in, far_ext,
           wgu, wdn, zsend, zrecv,
           load_sem, n_s, n_r, x_s, x_r, y_s, y_r, p_s, p_r, u_s, u_r, f_s, f_r, z_s, z_r):
    ex, et = lax.axis_index("exp"), lax.axis_index("et")
    y, core = ex // 2, ex % 2
    x, z = et // NZ, et % NZ
    odd = z % 2
    own_at = pl.multiple_of(WB + odd * WO, WO)
    other_at = pl.multiple_of(WB + (1 - odd) * WO, WO)
    column = x * 2 + z // 16
    expert = ex * 8 + column

    def at_z(dz):
        return (ex, x * NZ + lax.rem(z + dz + NZ, NZ))

    def at_x(dx):
        return (ex, lax.rem(x + dx, NX) * NZ + z)

    def exp_of(step):
        dy, dc = step
        return lax.rem(y + dy, 4) * 2 + lax.rem(core + dc, 2)

    def send(src, dst, ss, rs, device):
        copy = pltpu.make_async_remote_copy(
            src_ref=src, dst_ref=dst, send_sem=ss, recv_sem=rs, device_id=device, device_id_type=MESH)
        copy.start()
        return copy

    sent = []
    used = [0]

    def z_copy(src, dst, dz):
        i = used[0]
        used[0] += 1
        return send(src, dst, n_s.at[i], n_r.at[i], at_z(dz))

    def arrived(copies):
        for copy in copies:
            copy.wait_recv()
        sent.extend(copies)

    barrier = pltpu.get_barrier_semaphore()
    partners = [at_z(d) for d in (4, -4, 3, -3, 2, -2, 1, -1)]
    partners += [at_x(d) for d in (1, 2, 3)]
    partners += [(exp_of(step), et) for step in EXP_STEPS]
    for device in partners:
        pl.semaphore_signal(barrier, inc=1, device_id=device, device_id_type=MESH)

    early = [pltpu.make_async_copy(src, dst, load_sem.at[i]) for i, (src, dst) in enumerate(
        ((grad_in, grad), (weights_in, weights), (ids_in, ids), (places_in, places)))]
    loads = [pltpu.make_async_copy(pre_in, pre, load_sem.at[4])]
    for i, (src, dst, row) in enumerate(((gate_hbm, wgu, 0), (up_hbm, wgu, 128), (down_hbm, wdn, 0))):
        for j, (at, to, width) in enumerate(((own_at, 0, WO), (0, WO, WB), (other_at, WO + WB, WO))):
            loads.append(pltpu.make_async_copy(
                src.at[0, :, pl.ds(at, width)], dst.at[pl.ds(row, UNITS), pl.ds(to, width)],
                load_sem.at[8 + i * 3 + j]))
    for load in early + loads:
        load.start()
    for load in early:
        load.wait()
    for i in range(D // 128):
        frows[i:i + 1, :] = grad[0:1, i * 128:(i + 1) * 128].astype(F32)
    tokens[0, :, 3] = frows[0:32].reshape(2, 16, 128).astype(BF)
    extras[0, 3] = jnp.concatenate(
        [ids[...].astype(F32), places[...].astype(F32), weights[...].astype(F32),
         jnp.zeros((1, EXT - 3 * TOPK), F32)], axis=1)
    near_in[2, 1, 0] = jnp.zeros((16, 128), BF)
    pad = jnp.zeros((32, D), BF)
    wgu[pl.ds(UNITS, 32)] = pad
    wgu[pl.ds(128 + UNITS, 32)] = pad
    wdn[pl.ds(UNITS, 32)] = pad
    pl.semaphore_wait(barrier, len(partners))

    def feats(h, cls, at, to_cls, to, count, dz):
        return z_copy(tokens.at[cls, h, pl.ds(at, count)], tokens.at[to_cls, h, pl.ds(to, count)], dz)

    def sides(cls, at, to_cls, to, count, dz):
        return z_copy(extras.at[cls, pl.ds(at, count)], extras.at[to_cls, pl.ds(to, count)], dz)

    def move(h, moves):
        return [feats(h, *m) for m in moves] + ([sides(*m) for m in moves] if h else [])

    halves = (1, 0)
    quarter = {h: move(h, [(0, 3, 0, 2, 1, 4), (0, 3, 0, 4, 1, -4)]) for h in halves}
    eighths, near = {}, {}
    for h in halves:
        arrived(quarter[h])
        eighths[h] = move(h, [(0, 3, 0, 5, 2, -8), (0, 2, 0, 0, 2, 8)])

    for h in halves:
        arrived(eighths[h])
        near[h] = move(h, [(0, 6, 0, 7, 1, -4), (0, 0, 1, 7, 1, 3), (0, 6, 3, 7, 1, -3), (0, 0, 2, 7, 1, 2),
                           (0, 0, 1, 0, 7, -1), (0, 0, 3, 0, 7, 1)])
        if h:
            near[h] += [feats(h, 0, 1, 2, 0, 6, 2), feats(h, 0, 6, 2, 6, 1, -2), sides(0, 0, 2, 0, 7, -2)]
        else:
            near[h] += [feats(h, 0, 0, 2, 0, 7, -2)]

    def spread_rows(h):
        arrived(near[h])
        for d in range(4):
            frows[(d * 2 + h) * 128:(d * 2 + h + 1) * 128] = tokens[d, h].astype(F32).reshape(128, 128)

    spread_rows(1)
    for d in range(4):
        for i in range(8):
            ext_rows[d * 8 + i:d * 8 + i + 1, :] = extras[d, i]
    g[0:32, 0:EXT] = ext_rows[...].astype(BF)
    gathers = []

    def unit(u):
        return jnp.concatenate(
            [frows[pl.ds((d * 2 + u // 16) * 128 + u % 16, 8, stride=16), :] for d in range(4)], axis=0)

    for f, (start, width) in enumerate(CUTS):
        begin, end = features(f)
        if f == 2:
            spread_rows(0)
        for col in range(begin, end, 128):
            v = (col - EXT) // 128
            if v < OWN:
                row = jnp.where(odd == 0, unit(BOTH + v), unit(BOTH + OWN + v))
            else:
                row = unit(v - OWN)
            g[0:32, col:col + 128] = row.astype(BF)
        cols = pl.ds(start, width)
        gathers.append([
            send(g.at[pl.ds(0, 32), cols], g.at[pl.ds((4 - dx) * 32, 32), cols],
                 x_s.at[dx - 1, f], x_r.at[dx - 1, f], at_x(dx))
            for dx in (1, 2, 3)])

    mine_rows = pl.ds(pl.multiple_of(ex * PAD, PAD), PAD)
    dispatch = []
    for f, (start, width) in enumerate(CUTS):
        cols = pl.ds(start, width)
        for copy in gathers[f]:
            copy.wait_recv()
        if f == 0:
            ext = g[:, 0:EXT].astype(F32)
            code = ext * 32.0 + pltpu.roll(ext, EXT - TOPK, 1)
            lane = lax.broadcasted_iota(jnp.int32, (128, ROWS), 1)
            target = ((lane // PAD) * 256 + lane % PAD + column * PAD).astype(F32)
            hit = jnp.zeros((128, ROWS), F32)
            for k in range(TOPK):
                hit = hit + jnp.where(code[:, k:k + 1] == target, 1.0, 0.0)
            st[...] = hit.astype(BF)
            s[...] = jnp.transpose(hit).astype(BF)
        ysend[:, start:start + width] = dot(s[...], g[:, start:start + width]).astype(BF)
        copies = []
        for j, step in enumerate(EXP_STEPS):
            to = exp_of(step)
            rows = pl.ds(pl.multiple_of(to * PAD, PAD), PAD)
            copies.append(send(ysend.at[rows, cols], yrecv.at[mine_rows, cols],
                               y_s.at[j, f], y_r.at[j, f], (to, et)))
        yrecv[mine_rows, start:start + width] = ysend[mine_rows, start:start + width]
        dispatch.append(copies)

    for load in loads:
        load.wait()
    slot_row = lax.broadcasted_iota(jnp.int32, (ROWS, SLOTS), 0)
    slot_col = lax.broadcasted_iota(jnp.int32, (ROWS, SLOTS), 1)
    place = (slot_row // PAD) * CAP + slot_row % PAD
    spread = jnp.where((place == slot_col) & (slot_row % PAD < CAP), 1.0, 0.0).astype(BF)
    pre_rows = dot(spread, pre[0], ((1,), (1,))).astype(BF)
    unit_row = lax.broadcasted_iota(jnp.int32, (2 * UNITS, 128), 0)
    unit_col = lax.broadcasted_iota(jnp.int32, (2 * UNITS, 128), 1)
    pick_gate = jnp.where((unit_row == unit_col) & (unit_col < UNITS), 1.0, 0.0).astype(BF)
    pick_up = jnp.where((unit_row == unit_col + UNITS) & (unit_col < UNITS), 1.0, 0.0).astype(BF)
    gate_pre = dot(pre_rows, pick_gate)
    up_pre = dot(pre_rows, pick_up)
    sig = jax.nn.sigmoid(gate_pre)
    active = gate_pre * sig
    product = active * up_pre
    hidden = product.astype(BF).astype(F32)
    gate_factor = up_pre * sig * (1.0 + gate_pre * (1.0 - sig))

    pair = at_z(1 - 2 * odd)
    forwards = []
    back = jnp.zeros((ROWS, 128), F32)
    for f in range(NCH):
        begin, end = features(f)
        for copy in dispatch[f]:
            copy.wait_recv()
        if f < 2:
            forwards.append(send(
                yrecv.at[:, pl.ds(begin, end - begin)], yrecv.at[:, pl.ds(WIDE + PARTS[f][0], end - begin)],
                f_s.at[f], f_r.at[f], pair))
        back = back + dot(yrecv[:, begin:end], wdn[:, begin - EXT:end - EXT], ((1,), (1,)))
        sent += dispatch[f] + gathers[f]
    for f in range(2):
        forwards[f].wait_recv()
        begin, end = WIDE + PARTS[f][0], WIDE + sum(PARTS[f])
        back = back + dot(yrecv[:, begin:end], wdn[:, begin - EXT:end - EXT], ((1,), (1,)))
    sent += forwards

    ext = yrecv[:, 0:EXT].astype(F32)
    lane = lax.broadcasted_iota(jnp.int32, (ROWS, EXT), 1)
    named = (lane < TOPK) & (ext.astype(jnp.int32) == expert)
    weight = jnp.sum(jnp.where(named, pltpu.roll(ext, EXT - 2 * TOPK, 1), 0.0), axis=1, keepdims=True)
    scaled = weight * back
    grads = jnp.concatenate([scaled * gate_factor, scaled * active], axis=1).astype(BF)
    part_prob = jnp.sum(hidden * back, axis=1, keepdims=True)
    psend[:, 0:EXT] = jnp.where(named, part_prob, 0.0).astype(BF)
    weighted = jnp.transpose(weight * product).astype(BF)

    swaps = {}
    for f in (1, 0):
        at, width = PARTS[f]
        begin = WO + WB + at
        zsend[:, at:at + width] = dot(grads, wgu[:, begin:begin + width]).astype(BF)
        part = pl.ds(at, width)
        swaps[f] = send(zsend.at[:, part], zrecv.at[:, part], z_s.at[f], z_r.at[f], pair)
    combine = [None] * NCH
    for f in BACK_ORDER:
        start, width = CUTS[f]
        begin, end = features(f)
        cols = pl.ds(start, width)
        part = dot(grads, wgu[:, begin - EXT:end - EXT])
        if f < 2:
            swaps[f].wait_recv()
            part = part + zrecv[:, PARTS[f][0]:sum(PARTS[f])].astype(F32)
        psend[:, begin:end] = part.astype(BF)
        copies = []
        for j, step in enumerate(EXP_STEPS):
            to = exp_of(step)
            rows = pl.ds(pl.multiple_of(to * PAD, PAD), PAD)
            copies.append(send(psend.at[rows, cols], precv.at[mine_rows, cols],
                               p_s.at[j, f], p_r.at[j, f], (to, et)))
        precv[mine_rows, start:start + width] = psend[mine_rows, start:start + width]
        combine[f] = copies
        if f == 3:
            for at, begin, width in ((0, EXT + WO, WB), (own_at, EXT, WO), (other_at, WIDE, WO)):
                gdown[:, pl.ds(at, width)] = dot(weighted, yrecv[:, begin:begin + width])[0:UNITS].astype(BF)
    sent += swaps.values()
    stores = [pltpu.make_async_copy(gdown, down_out, load_sem.at[5])]
    stores[0].start()

    reduces = [None] * NCH

    def combine_rows(f):
        start, width = CUTS[f]
        cols = pl.ds(start, width)
        arrived(combine[f])
        dense = dot(st[...], precv[:, start:start + width])
        acc[:, start:start + width] = dense[0:32]
        xsend[:, start:start + width] = dense[32:128].astype(BF)
        reduces[f] = [
            send(xsend.at[pl.ds((dx - 1) * 32, 32), cols], xrecv.at[dx - 1, :, cols],
                 u_s.at[dx - 1, f], u_r.at[dx - 1, f], at_x(dx))
            for dx in (1, 2, 3)]

    def put(u, rows):
        for d in range(4):
            frows[pl.ds((d * 2 + u // 16) * 128 + u % 16, 8, stride=16), :] = rows[d * 8:d * 8 + 8]

    def sum_rows(f):
        start, width = CUTS[f]
        begin, end = features(f)
        arrived(reduces[f])
        whole = acc[:, start:start + width]
        for i in range(3):
            whole = whole + xrecv[i, :, start:start + width].astype(F32)
        if f == 0:
            for d in range(4):
                for i in range(8):
                    sum_ext[d, i] = whole[d * 8 + i:d * 8 + i + 1, 0:EXT]
        for col in range(begin, end, 128):
            v = (col - EXT) // 128
            rows = whole[:, col - start:col - start + 128]
            if v < OWN:
                put(BOTH + v, jnp.where(odd == 0, rows, 0.0))
                put(BOTH + OWN + v, jnp.where(odd == 0, 0.0, rows))
            else:
                put(v - OWN, rows)

    def send_near(h):
        for d in range(4):
            if d:
                sums[d, h] = frows[(d * 2 + h) * 128:(d * 2 + h + 1) * 128].reshape(8, 16, 128).astype(BF)
            else:
                sums[d, h, 7] = frows[h * 128 + 112:h * 128 + 128].astype(BF)
        copies = []
        for cls, to, dz in ((0, 3, 4), (1, 1, -3), (3, 2, 3), (2, 0, -2)):
            copies.append(z_copy(sums.at[cls, h, pl.ds(7, 1)], single_in.at[to, h], dz))
            if h:
                copies.append(z_copy(sum_ext.at[cls, pl.ds(7, 1)], single_ext.at[to], dz))
        for cls, to, dz in ((1, 0, 1), (3, 1, -1), (2, 2, 2)):
            if cls != 2 or h == 0:
                copies.append(z_copy(sums.at[cls, h, pl.ds(0, 7)], near_in.at[to, h, pl.ds(0, 7)], dz))
            if h:
                copies.append(z_copy(sum_ext.at[cls, pl.ds(0, 7)], near_ext.at[to], dz))
        if h:
            copies.append(z_copy(sums.at[2, 1, pl.ds(0, 6)], near_in.at[2, 1, pl.ds(1, 6)], -2))
            copies.append(z_copy(sums.at[2, 1, pl.ds(6, 1)], single_in.at[4, 1], 2))
        return copies

    combine_rows(2)
    combine_rows(3)
    combine_rows(1)
    sum_rows(2)
    sum_rows(3)
    near = {0: send_near(0)}
    combine_rows(0)
    sum_rows(1)
    sum_rows(0)
    near[1] = send_near(1)

    def send_far(h):
        arrived(near[h])
        rows = frows[h * 128:h * 128 + 112].reshape(7, 16, 128)
        for i in range(3):
            rows = rows + near_in[i, h, 0:7].astype(F32)
        total[h] = rows
        for place, left in ((0, (0, 1)), (6, (2, 3))):
            for i in left:
                total[h, place] = total[h, place] + single_in[i, h, 0].astype(F32)
        if h:
            total[1, 6] = total[1, 6] + single_in[4, 1, 0].astype(F32)
            rows = sum_ext[0, 0:7]
            for i in range(3):
                rows = rows + near_ext[i]
            total_ext[...] = rows
            for place, left in ((0, (0, 1)), (6, (2, 3))):
                for i in left:
                    total_ext[place] = total_ext[place] + single_ext[i, 0]
        far_send[h] = total[h].astype(BF)
        copies = []
        for at, to, dz in ((5, 0, 8), (0, 1, -8)):
            copies.append(z_copy(far_send.at[h, pl.ds(at, 2)], far_in.at[to, h], dz))
            if h:
                copies.append(z_copy(total_ext.at[pl.ds(at, 2)], far_ext.at[to], dz))
        return copies

    far = {h: send_far(h) for h in (0, 1)}

    def send_last(h):
        arrived(far[h])
        far_send[h, 2] = (total[h, 2] + far_in[1, h, 0].astype(F32)).astype(BF)
        far_send[h, 4] = (total[h, 4] + far_in[0, h, 1].astype(F32)).astype(BF)
        total[h, 3] = total[h, 3] + far_in[0, h, 0].astype(F32) + far_in[1, h, 1].astype(F32)
        if h:
            total_ext[2] = total_ext[2] + far_ext[1, 0]
            total_ext[4] = total_ext[4] + far_ext[0, 1]
            total_ext[3] = total_ext[3] + far_ext[0, 0] + far_ext[1, 1]
        copies = []
        for at, to, dz in ((2, 2, -4), (4, 3, 4)):
            copies.append(z_copy(far_send.at[h, pl.ds(at, 1)], far_in.at[to, h, pl.ds(0, 1)], dz))
            if h:
                copies.append(z_copy(total_ext.at[pl.ds(at, 1)], far_ext.at[to, pl.ds(0, 1)], dz))
        return copies

    last = {h: send_last(h) for h in (0, 1)}
    for h in (0, 1):
        arrived(last[h])
        frows[h * 16:h * 16 + 16] = total[h, 3] + far_in[2, h, 0].astype(F32) + far_in[3, h, 0].astype(F32)
    for i in range(D // 128):
        tok[0:1, i * 128:(i + 1) * 128] = frows[i:i + 1, :].astype(BF)
    prob[...] = (total_ext[3] + far_ext[2, 0] + far_ext[3, 0])[:, 0:TOPK]
    for i, (src, dst) in enumerate(((tok, tok_out), (prob, prob_out))):
        stores.append(pltpu.make_async_copy(src, dst, load_sem.at[6 + i]))
        stores[-1].start()
    for copy in sent:
        copy.wait_send()
    for store in stores:
        store.wait()


def deliver(tok, prob, down, tok_out, prob_out, down_out, tok_buf, prob_buf, down_buf, in_sem, out_sem):
    parts = [(tok, tok_buf, tok_out), (prob, prob_buf, prob_out)]
    for i in range(0, UNITS, 32):
        rows = pl.ds(i, 32)
        parts.append((down.at[rows], down_buf.at[rows], down_out.at[rows]))
    ins = [pltpu.make_async_copy(src, buf, in_sem.at[i]) for i, (src, buf, _) in enumerate(parts)]
    outs = [pltpu.make_async_copy(buf, dst, out_sem.at[i]) for i, (_, buf, dst) in enumerate(parts)]
    for copy in ins:
        copy.start()
    for copy, onward in zip(ins, outs):
        copy.wait()
        onward.start()
    for copy in outs:
        copy.wait()


def body(grad_out, route_weight, expert_ids, slot_ids, saved_pre, gate_proj, up_proj, down_proj):
    hbm = pl.BlockSpec(memory_space=pl.ANY)
    dma = lambda *shape: pltpu.SemaphoreType.DMA(shape)
    outs = (
        jax.ShapeDtypeStruct((1, D), BF),
        jax.ShapeDtypeStruct((1, TOPK), F32),
        jax.ShapeDtypeStruct((UNITS, D), BF),
    )
    results = pl.pallas_call(
        kernel,
        out_shape=outs,
        in_specs=[hbm] * 8,
        out_specs=(hbm,) * 3,
        scratch_shapes=[
            pltpu.VMEM((1, D), BF),
            pltpu.VMEM((1, TOPK), BF),
            pltpu.VMEM((1, TOPK), jnp.int32),
            pltpu.VMEM((1, TOPK), jnp.int32),
            pltpu.VMEM((1, 2 * UNITS, SLOTS), BF),
            pltpu.VMEM((1, D), BF),
            pltpu.VMEM((1, TOPK), F32),
            pltpu.VMEM((UNITS, D), BF),
            pltpu.VMEM((4, 2, 8, 16, 128), BF),
            pltpu.VMEM((4, 8, 1, 128), F32),
            pltpu.VMEM((32, 128), F32),
            pltpu.VMEM((1024, 128), F32),
            pltpu.VMEM((128, WIDE), BF),
            pltpu.VMEM((128, ROWS), BF),
            pltpu.VMEM((ROWS, 128), BF),
            pltpu.VMEM((ROWS, WIDE), BF),
            pltpu.VMEM((ROWS, EXT + D), BF),
            pltpu.VMEM((ROWS, WIDE), BF),
            pltpu.VMEM((ROWS, WIDE), BF),
            pltpu.VMEM((96, WIDE), BF),
            pltpu.VMEM((3, 32, WIDE), BF),
            pltpu.VMEM((32, WIDE), F32),
            pltpu.VMEM((4, 2, 8, 16, 128), BF),
            pltpu.VMEM((4, 8, 1, 128), F32),
            pltpu.VMEM((3, 2, 7, 16, 128), BF),
            pltpu.VMEM((3, 7, 1, 128), F32),
            pltpu.VMEM((5, 2, 1, 16, 128), BF),
            pltpu.VMEM((4, 1, 1, 128), F32),
            pltpu.VMEM((2, 7, 16, 128), F32),
            pltpu.VMEM((7, 1, 128), F32),
            pltpu.VMEM((2, 7, 16, 128), BF),
            pltpu.VMEM((4, 2, 2, 16, 128), BF),
            pltpu.VMEM((4, 2, 1, 128), F32),
            pltpu.VMEM((256, D), BF),
            pltpu.VMEM((128, D), BF),
            pltpu.VMEM((ROWS, WO), BF),
            pltpu.VMEM((ROWS, WO), BF),
            dma(17), dma(96), dma(96), dma(3, NCH), dma(3, NCH), dma(7, NCH), dma(7, NCH),
            dma(7, NCH), dma(7, NCH), dma(3, NCH), dma(3, NCH),
            dma(2), dma(2), dma(2), dma(2),
        ],
        compiler_params=pltpu.CompilerParams(
            collective_id=0, has_side_effects=True, vmem_limit_bytes=60 * 2**20),
    )(grad_out, route_weight, expert_ids, slot_ids, jnp.swapaxes(saved_pre, 1, 2), gate_proj, up_proj, down_proj)
    tokens, probs, down_grad = pl.pallas_call(
        deliver,
        out_shape=outs,
        in_specs=[hbm] * 3,
        out_specs=(hbm,) * 3,
        scratch_shapes=[
            pltpu.VMEM((1, D), BF), pltpu.VMEM((1, TOPK), F32), pltpu.VMEM((UNITS, D), BF), dma(5), dma(5)],
    )(*results)
    return tokens, probs, down_grad[None]


def solution(mesh):
    rows, blocks = P(("exp", "et"), None), P(("exp", "et"), None, None)
    return jax.shard_map(
        body, mesh=mesh, in_specs=(rows, rows, rows, rows, blocks, blocks, blocks, blocks),
        out_specs=(rows, rows, blocks), check_vma=False)
```
